512 devices in a mesh: seq: 128 (over z_hi, y, x), mp: 4 (over z_lo, core).
Axes of the slice: x: 4, y: 8, z: 8 (z_hi: 4, z_lo: 2; z = z_hi * 2 + z_lo), core: 2. Of those that a mesh axis runs over, the one named last changes fastest.
Arguments:
- queries: bfloat16 [65536, 2048], P('seq', 'mp'), may hold values from -24 to 24
- keys: bfloat16 [65536, 2048], P('seq', 'mp'), may hold values from -24 to 24
- values: bfloat16 [65536, 2048], P('seq', 'mp'), may hold values from -6 to 6
- out_weight: bfloat16 [2048, 4096], P('mp', 'seq'), may hold values from -0.125 to 0.125
Outputs:
- layer_out: bfloat16 [65536, 4096], P('seq', 'mp')
The draws below stay inside these ranges and needn't reach their ends.
All inputs are finite; a program needn't handle non-finite values.
Results may differ from the reference program's by a relative error of at most 0.013.
Values may be sent and summed in bfloat16 or wider, within the bound.
No kernel may reach another device: no remote copies, remote signals or barrier semaphores. Data moves between devices by JAX's collectives and lax.ppermute only.
A program may use at most 64 MiB of HBM per device.

```python
import jax
import jax.numpy as jnp
from jax import lax

D = 4096
HEADS = 16
DH = 128
STRIDE = 1024
TOKENS = 65536
N_MP = 4


def draw_queries(key, part):
    key = jax.random.fold_in(key, 1)
    base = jnp.clip(jax.random.normal(key, (TOKENS, HEADS * DH), jnp.float32), -5.0, 5.0)
    return base.astype(jnp.bfloat16)


def draw_keys(key, part):
    key = jax.random.fold_in(key, 7)
    base = jnp.clip(jax.random.normal(key, (TOKENS, HEADS * DH), jnp.float32), -5.0, 5.0)
    return base.astype(jnp.bfloat16)


def block_levels(own_key, shape, shards, smallest, largest):
    factor_of = 1.0
    for dim, parts in shards:
        heights = jax.random.uniform(jax.random.fold_in(jax.random.fold_in(own_key, 6), dim), (parts,), jnp.float32, smallest / len(shards), largest / len(shards))
        factor_of = factor_of * jnp.repeat(jnp.exp(heights), shape[dim] // parts).reshape((-1,) + (1,) * (len(shape) - 1 - dim))
    return factor_of


def bell_draw(stream_key, dims, scale, most, split=(), kind=jnp.bfloat16):
    gain = block_levels(stream_key, dims, split, -0.22, 0.18) if split else 1.0
    values = jax.random.normal(stream_key, dims, jnp.float32) * scale * gain
    return jnp.minimum(jnp.maximum(values, -most), most).astype(kind)


def setup_inputs(seed: int = 0) -> dict:
    arg_keys = jax.random.split(jax.random.key(seed), 5)
    queries = draw_queries(jax.random.fold_in(arg_keys[4], 71), 0)
    keys = draw_keys(jax.random.fold_in(arg_keys[4], 71), 0)
    values = bell_draw(arg_keys[2], (TOKENS, HEADS * DH), 1.0, 6.0, ((0, 128), (1, 4)))
    out_weight = bell_draw(arg_keys[3], (HEADS * DH, D), (HEADS * DH) ** -0.5, 0.125, ((0, 4), (1, 128)))
    return {"queries": queries, "keys": keys, "values": values, "out_weight": out_weight}


def column_block(arrays):
    query_col, key_col, value_col = arrays
    row_count = query_col.shape[0]
    factor = DH ** -0.5
    scores = jnp.einsum('rchd,schd->rchs', query_col.astype(jnp.float32), key_col.astype(jnp.float32)) * factor
    earlier_row = jnp.arange(row_count)[None, :] < jnp.arange(row_count)[:, None]
    visible = earlier_row[:, None, None, :]
    col_max = jnp.max(jnp.where(visible, scores, jnp.float32(-1e30)), axis=-1)
    col_exp = jnp.where(visible, jnp.exp(scores - col_max[..., None]), jnp.float32(0.0))
    col_total = jnp.sum(col_exp, axis=-1)
    weights = lax.optimization_barrier(col_exp.astype(jnp.bfloat16)).astype(jnp.float32)
    col_out = jnp.einsum('rchs,schd->rchd', weights, value_col.astype(jnp.float32))
    return col_out, col_max, col_total


def reference(queries, keys, values, out_weight):
    factor = DH ** -0.5
    row_count = TOKENS // STRIDE
    group = min(64, STRIDE)
    width = HEADS * DH

    def by_columns(field):
        return jnp.moveaxis(field.reshape(row_count, STRIDE // group, group, HEADS, DH), 1, 0)

    col_out, col_max, col_total = lax.map(column_block, (by_columns(queries), by_columns(keys), by_columns(values)))
    col_out = jnp.moveaxis(col_out, 0, 1).reshape(row_count, STRIDE, HEADS, DH)
    col_max = jnp.moveaxis(col_max, 0, 1).reshape(row_count, STRIDE, HEADS)
    col_total = jnp.moveaxis(col_total, 0, 1).reshape(row_count, STRIDE, HEADS)
    weight_groups = out_weight.reshape(N_MP, width // N_MP, D)

    def row_block(arrays):
        query_blk, key_blk, value_blk, col_out_blk, col_max_blk, col_total_blk = arrays
        query_heads = query_blk.reshape(STRIDE, HEADS, DH).astype(jnp.float32)
        key_heads = key_blk.reshape(STRIDE, HEADS, DH).astype(jnp.float32)
        value_heads = value_blk.reshape(STRIDE, HEADS, DH).astype(jnp.float32)
        scores = jnp.einsum('qhd,khd->qhk', query_heads, key_heads) * factor
        positions = jnp.arange(STRIDE)
        visible = (positions[None, :] <= positions[:, None])[:, None, :]
        row_max = jnp.max(jnp.where(visible, scores, jnp.float32(-1e30)), axis=-1)
        row_exp = jnp.where(visible, jnp.exp(scores - row_max[..., None]), jnp.float32(0.0))
        row_total = jnp.sum(row_exp, axis=-1)
        weights = lax.optimization_barrier(row_exp.astype(jnp.bfloat16)).astype(jnp.float32)
        row_out = jnp.einsum('qhk,khd->qhd', weights, value_heads)
        highest = jnp.maximum(row_max, col_max_blk)
        row_factor = jnp.exp(row_max - highest)
        col_factor = jnp.exp(col_max_blk - highest)
        mixed = (row_factor[..., None] * row_out + col_factor[..., None] * col_out_blk) / (row_factor * row_total + col_factor * col_total_blk)[..., None]
        attended = mixed.astype(jnp.bfloat16).reshape(STRIDE, N_MP, width // N_MP)
        total = jnp.zeros((STRIDE, D), jnp.float32)
        for member in range(N_MP):
            partial_value = jnp.dot(attended[:, member], weight_groups[member], preferred_element_type=jnp.float32)
            rounded = lax.optimization_barrier(partial_value.astype(jnp.bfloat16))
            total = total + rounded.astype(jnp.float32)
        return total.astype(jnp.bfloat16)

    blocks = lax.map(row_block, (queries.reshape(row_count, STRIDE, width), keys.reshape(row_count, STRIDE, width), values.reshape(row_count, STRIDE, width), col_out, col_max, col_total))
    return blocks.reshape(TOKENS, D)
```

```python
import functools

import jax
import jax.numpy as jnp
from jax import lax
from jax.experimental import pallas as pl
from jax.experimental.pallas import tpu as pltpu
from jax.sharding import PartitionSpec as P

DH = 128
HEADS_HERE = 4
ROWS = 512
WIDTH = HEADS_HERE * DH
N_MP = 4
N_SEQ = 128
PLANE = 32
COLS = 8
NEG = -1e30
FACTOR = DH ** (-0.5)
VMEM = 40 * 1024 * 1024

NT = (((1,), (1,)), ((), ()))


def nt_dot(a, b):
    return lax.dot_general(a, b, NT, preferred_element_type=jnp.float32)


def three_parts(x):
    hi = x.astype(jnp.bfloat16).astype(jnp.float32)
    rest = x - hi
    mid = rest.astype(jnp.bfloat16).astype(jnp.float32)
    return hi, mid, rest - mid


def stat_lanes(old, head, largest, total):
    lane = lax.broadcasted_iota(jnp.int32, old.shape, 1)
    out = old
    for place, part in enumerate(three_parts(largest) + three_parts(total)):
        out = jnp.where(lane == head + 4 * place, part, out)
    return out


def spread_stats(stats):
    lane = lax.broadcasted_iota(jnp.int32, (128, WIDTH), 0)
    head = lax.broadcasted_iota(jnp.int32, (128, WIDTH), 1) // DH
    mine = (lane % 4) == head
    pick_max = jnp.where(mine & (lane < 12), 1.0, 0.0).astype(jnp.bfloat16)
    pick_total = jnp.where(mine & (lane >= 12) & (lane < 24), 1.0, 0.0).astype(jnp.bfloat16)
    largest = jnp.dot(stats, pick_max, preferred_element_type=jnp.float32)
    total = jnp.dot(stats, pick_total, preferred_element_type=jnp.float32)
    return largest, total


def row_kernel(parity_ref, q_ref, k_ref, v_ref, kp_ref, vp_ref, out_ref, stat_ref):
    head = pl.program_id(0)
    odd = parity_ref[0] == 1
    block = 128

    @pl.when(head == 0)
    def _():
        stat_ref[...] = jnp.zeros_like(stat_ref)

    for b in range(ROWS // block):
        here = slice(b * block, (b + 1) * block)
        seen = (b + 1) * block
        q = q_ref[here, :]
        own = nt_dot(q, k_ref[:seen, :]) * FACTOR
        place = lax.broadcasted_iota(jnp.int32, (block, seen), 0) + b * block
        other = lax.broadcasted_iota(jnp.int32, (block, seen), 1)
        own = jnp.where(other <= place, own, NEG)
        before = nt_dot(q, kp_ref[...]) * FACTOR
        before = jnp.where(odd, before, NEG)
        largest = jnp.maximum(
            jnp.max(own, axis=1, keepdims=True), jnp.max(before, axis=1, keepdims=True)
        )
        own = jnp.exp(own - largest)
        before = jnp.exp(before - largest)
        total = jnp.sum(own, axis=1, keepdims=True) + jnp.sum(before, axis=1, keepdims=True)
        out_ref[here, :] = jnp.dot(
            own.astype(jnp.bfloat16), v_ref[:seen, :], preferred_element_type=jnp.float32
        ) + jnp.dot(before.astype(jnp.bfloat16), vp_ref[...], preferred_element_type=jnp.float32)
        stat_ref[here, :] = stat_lanes(
            stat_ref[here, :].astype(jnp.float32), head, largest, total
        ).astype(jnp.bfloat16)


def row_attend(parity, q, k, v, kp, vp):
    per_head = pl.BlockSpec((ROWS, DH), lambda h, s: (0, h))
    return pl.pallas_call(
        row_kernel,
        out_shape=(
            jax.ShapeDtypeStruct((ROWS, WIDTH), jnp.float32),
            jax.ShapeDtypeStruct((ROWS, 128), jnp.bfloat16),
        ),
        grid_spec=pltpu.PrefetchScalarGridSpec(
            num_scalar_prefetch=1,
            grid=(HEADS_HERE,),
            in_specs=[per_head] * 5,
            out_specs=(per_head, pl.BlockSpec((ROWS, 128), lambda h, s: (0, 0))),
        ),
        compiler_params=pltpu.CompilerParams(vmem_limit_bytes=VMEM),
        cost_estimate=pl.CostEstimate(
            flops=2 * 2 * 4 * ROWS * 2 * ROWS * DH,
            bytes_accessed=5 * 1024 * 1024,
            transcendentals=4 * ROWS * 2 * ROWS,
        ),
        name="row_attend",
    )(parity, q, k, v, kp, vp)


def col_kernel(q_ref, k_ref, v_ref, out_ref):
    head = pl.program_id(0)
    block = 128
    stat_place = slice(WIDTH, WIDTH + 128)

    @pl.when(head == 0)
    def _():
        out_ref[:, stat_place] = jnp.zeros((ROWS, 128), jnp.bfloat16)

    for b in range(ROWS // block):
        here = slice(b * block, (b + 1) * block)
        seen = (b + 1) * block
        scores = nt_dot(q_ref[here, :], k_ref[:seen, :]) * FACTOR
        token = lax.broadcasted_iota(jnp.int32, (block, seen), 0) + b * block
        other = lax.broadcasted_iota(jnp.int32, (block, seen), 1)
        visible = (other < token) & ((token & (COLS - 1)) == (other & (COLS - 1)))
        largest = jnp.max(jnp.where(visible, scores, NEG), axis=1, keepdims=True)
        weights = jnp.where(visible, jnp.exp(scores - largest), 0.0)
        total = jnp.sum(weights, axis=1, keepdims=True)
        out = jnp.dot(
            weights.astype(jnp.bfloat16), v_ref[:seen, :], preferred_element_type=jnp.float32
        )
        out_ref[here, pl.ds(pl.multiple_of(head * DH, DH), DH)] = out.astype(jnp.bfloat16)
        out_ref[here, stat_place] = stat_lanes(
            out_ref[here, stat_place].astype(jnp.float32), head, largest, total
        ).astype(jnp.bfloat16)


def col_attend(qkv):
    def third(n):
        return pl.BlockSpec((ROWS, DH), lambda h: (0, HEADS_HERE * n + h))

    return pl.pallas_call(
        col_kernel,
        out_shape=jax.ShapeDtypeStruct((ROWS, WIDTH + 128), jnp.bfloat16),
        grid=(HEADS_HERE,),
        in_specs=[third(0), third(1), third(2)],
        out_specs=pl.BlockSpec((ROWS, WIDTH + 128), lambda h: (0, 0)),
        compiler_params=pltpu.CompilerParams(vmem_limit_bytes=VMEM),
        cost_estimate=pl.CostEstimate(
            flops=2 * 2 * 4 * ROWS * ROWS * DH,
            bytes_accessed=2 * 1024 * 1024,
            transcendentals=4 * ROWS * ROWS,
        ),
        name="col_attend",
    )(qkv, qkv, qkv)


def mix_kernel(row_ref, row_stat_ref, col_ref, out_ref):
    row_max, row_total = spread_stats(row_stat_ref[...])
    col_max, col_total = spread_stats(col_ref[:, WIDTH : WIDTH + 128])
    highest = jnp.maximum(row_max, col_max)
    row_factor = jnp.exp(row_max - highest)
    col_factor = jnp.exp(col_max - highest)
    mixed = row_factor * row_ref[...] + col_factor * col_ref[:, :WIDTH].astype(jnp.float32)
    out_ref[...] = (mixed / (row_factor * row_total + col_factor * col_total)).astype(jnp.bfloat16)


def mix(row_out, row_stat, col):
    block = 128

    def rows(width):
        return pl.BlockSpec((block, width), lambda i: (i, 0))

    return pl.pallas_call(
        mix_kernel,
        out_shape=jax.ShapeDtypeStruct((ROWS, WIDTH), jnp.bfloat16),
        grid=(ROWS // block,),
        in_specs=[rows(WIDTH), rows(128), rows(WIDTH + 128)],
        out_specs=rows(WIDTH),
        compiler_params=pltpu.CompilerParams(vmem_limit_bytes=VMEM),
        cost_estimate=pl.CostEstimate(
            flops=4 * 2 * ROWS * 128 * WIDTH,
            bytes_accessed=3 * 1024 * 1024,
            transcendentals=2 * ROWS * WIDTH,
        ),
        name="mix",
    )(row_out, row_stat, col)


def project_kernel(order_ref, a0, a1, a2, a3, w0, w1, w2, w3, out_ref):
    total = None
    for a_ref, w_ref in ((a0, w0), (a1, w1), (a2, w2), (a3, w3)):
        weight = w_ref[...].reshape(out_ref.shape[1], WIDTH)
        term = nt_dot(a_ref[...], weight)
        total = term if total is None else total + term
    out_ref[...] = total.astype(jnp.bfloat16)


def project(order, attended, gathered):
    steps = 4
    here = PLANE // steps
    whole = pl.BlockSpec((ROWS, WIDTH), lambda i, s: (0, 0))

    def weight(j):
        return pl.BlockSpec((here, 1, 32, WIDTH), lambda i, s: (i, s[j], 0, 0))

    return pl.pallas_call(
        project_kernel,
        out_shape=jax.ShapeDtypeStruct((ROWS, PLANE * 32), jnp.bfloat16),
        grid_spec=pltpu.PrefetchScalarGridSpec(
            num_scalar_prefetch=1,
            grid=(steps,),
            in_specs=[whole] * 4 + [weight(j) for j in range(4)],
            out_specs=pl.BlockSpec((ROWS, here * 32), lambda i, s: (0, i)),
        ),
        compiler_params=pltpu.CompilerParams(vmem_limit_bytes=VMEM),
        cost_estimate=pl.CostEstimate(
            flops=2 * ROWS * 4 * WIDTH * PLANE * 32,
            bytes_accessed=7 * 1024 * 1024,
            transcendentals=0,
        ),
        name="project",
    )(order, *attended, gathered, gathered, gathered, gathered)


def same_parity():
    return [[i for i in range(N_SEQ) if i % 2 == p] for p in range(2)]


def swap_columns(value):
    return lax.all_to_all(
        value, "seq", split_axis=0, concat_axis=0, axis_index_groups=same_parity(), tiled=True
    )


def gather_weight(out_weight):
    mine = out_weight.T
    slots = []
    for k in range(N_MP):
        pairs = []
        for seq in range(N_SEQ):
            for mp in range(N_MP):
                z, place = divmod(seq, PLANE)
                target = ((mp + k) % N_MP) * PLANE + place
                pairs.append((seq * N_MP + mp, target * N_MP + z))
        slots.append(lax.ppermute(mine, ("seq", "mp"), pairs))
    stacked = jnp.concatenate(slots, axis=0)
    planes = [[z * PLANE + i for i in range(PLANE)] for z in range(N_MP)]
    gathered = lax.all_gather(stacked, "seq", axis=0, axis_index_groups=planes, tiled=True)
    return gathered.reshape(PLANE, N_MP, 32, WIDTH)


def body(queries, keys, values, out_weight):
    seq, mp = lax.axis_index("seq"), lax.axis_index("mp")
    arrived = swap_columns(jnp.concatenate([queries, keys, values], axis=1))
    gathered = gather_weight(out_weight)

    to_odd = [(i, i + 1) for i in range(0, N_SEQ, 2)]
    keys_before = lax.ppermute(keys, "seq", to_odd)
    values_before = lax.ppermute(values, "seq", to_odd)
    row_out, row_stat = row_attend(
        (seq % 2).astype(jnp.int32).reshape(1), queries, keys, values, keys_before, values_before
    )

    col = swap_columns(col_attend(arrived))
    attended = mix(row_out, row_stat, col)

    near = [(i, i ^ 1) for i in range(N_MP)]
    far = [(i, i ^ 2) for i in range(N_MP)]
    across = lax.ppermute(attended, "mp", far)
    beside = lax.ppermute(attended, "mp", near)
    last = lax.ppermute(across, "mp", near)
    z = seq // PLANE
    order = jnp.stack([(z - (mp ^ j)) % N_MP for j in range(N_MP)]).astype(jnp.int32)
    return project(order, (attended, beside, across, last), gathered)


def solution(mesh):
    placed = (P("seq", "mp"), P("seq", "mp"), P("seq", "mp"), P("mp", "seq"))
    return jax.shard_map(
        body, mesh=mesh, in_specs=placed, out_specs=P("seq", "mp"), check_vma=False
    )
```

```python
import functools

import jax
import jax.numpy as jnp
from jax import lax
from jax.experimental import pallas as pl
from jax.experimental.pallas import tpu as pltpu
from jax.sharding import PartitionSpec as P

DH = 128
HEADS_HERE = 4
ROWS = 512
WIDTH = HEADS_HERE * DH
N_MP = 4
N_SEQ = 128
PLANE = 32
COLS = 8
NEG = -1e30
NONE = -1e29
FACTOR = DH ** (-0.5) * 1.4426950408889634
VMEM = 40 * 1024 * 1024
SMALL = pl.CostEstimate(flops=1024, bytes_accessed=1024, transcendentals=0)

NT = (((1,), (1,)), ((), ()))


def nt_dot(a, b):
    return lax.dot_general(a, b, NT, preferred_element_type=jnp.float32)


def stat_lanes(old, head, largest, total):
    lane = lax.broadcasted_iota(jnp.int32, old.shape, 1)
    return jnp.where(lane == head, largest, jnp.where(lane == 4 + head, total, old))


def three_parts(stats):
    high = stats.astype(jnp.bfloat16).astype(jnp.float32)
    rest = stats - high
    middle = rest.astype(jnp.bfloat16).astype(jnp.float32)
    low = rest - middle
    parts = high + pltpu.roll(middle, 8, 1) + pltpu.roll(low, 16, 1)
    return parts.astype(jnp.bfloat16)


def spread_stats(stats):
    lane = lax.broadcasted_iota(jnp.int32, (128, WIDTH), 0)
    head = lax.broadcasted_iota(jnp.int32, (128, WIDTH), 1) // DH
    kept = lane < 24
    pick_max = jnp.where(kept & ((lane & 7) == head), 1.0, 0.0).astype(jnp.bfloat16)
    pick_total = jnp.where(kept & ((lane & 7) == head + 4), 1.0, 0.0).astype(jnp.bfloat16)
    largest = jnp.dot(stats, pick_max, preferred_element_type=jnp.float32)
    total = jnp.dot(stats, pick_total, preferred_element_type=jnp.float32)
    return largest, total


def row_kernel(parity_ref, q_ref, k_ref, v_ref, kp_ref, vp_ref, out_ref, packed_ref, stat_ref):
    head = pl.program_id(0)
    odd = parity_ref[0] == 1
    block = 128

    @pl.when(head == 0)
    def _():
        stat_ref[...] = jnp.zeros_like(stat_ref)

    for b in range(ROWS // block):
        here = slice(b * block, (b + 1) * block)
        seen = (b + 1) * block
        q = q_ref[here, :]
        own = nt_dot(q, k_ref[:seen, :]) * FACTOR
        place = lax.broadcasted_iota(jnp.int32, (block, seen), 0) + b * block
        other = lax.broadcasted_iota(jnp.int32, (block, seen), 1)
        own = jnp.where(other <= place, own, NEG)
        before = nt_dot(q, kp_ref[...]) * FACTOR
        before = jnp.where(odd, before, NEG)
        largest = jnp.maximum(
            jnp.max(own, axis=1, keepdims=True), jnp.max(before, axis=1, keepdims=True)
        )
        own = jnp.exp2(own - largest)
        before = jnp.exp2(before - largest)
        total = jnp.sum(own, axis=1, keepdims=True) + jnp.sum(before, axis=1, keepdims=True)
        out_ref[here, :] = jnp.dot(
            own.astype(jnp.bfloat16), v_ref[:seen, :], preferred_element_type=jnp.float32
        ) + jnp.dot(before.astype(jnp.bfloat16), vp_ref[...], preferred_element_type=jnp.float32)
        stat_ref[here, :] = stat_lanes(stat_ref[here, :], head, largest, total)

    @pl.when(head == HEADS_HERE - 1)
    def _():
        packed_ref[...] = three_parts(stat_ref[...])


def row_attend(parity, q, k, v, kp, vp):
    per_head = pl.BlockSpec((ROWS, DH), lambda h, s: (0, h))
    return pl.pallas_call(
        row_kernel,
        out_shape=(
            jax.ShapeDtypeStruct((ROWS, WIDTH), jnp.float32),
            jax.ShapeDtypeStruct((ROWS, 128), jnp.bfloat16),
        ),
        grid_spec=pltpu.PrefetchScalarGridSpec(
            num_scalar_prefetch=1,
            grid=(HEADS_HERE,),
            in_specs=[per_head] * 5,
            out_specs=(per_head, pl.BlockSpec((ROWS, 128), lambda h, s: (0, 0))),
            scratch_shapes=[pltpu.VMEM((ROWS, 128), jnp.float32)],
        ),
        compiler_params=pltpu.CompilerParams(vmem_limit_bytes=VMEM),
        cost_estimate=SMALL,
        name="row_attend",
    )(parity, q, k, v, kp, vp)


def col_kernel(qkv_ref, out_ref):
    block = 128
    token = lax.broadcasted_iota(jnp.int32, (block, block), 0)
    other = lax.broadcasted_iota(jnp.int32, (block, block), 1)
    same = (token & (COLS - 1)) == (other & (COLS - 1))
    earlier = same & (other < token)
    for b in range(ROWS // block):
        here = slice(b * block, (b + 1) * block)
        stats = jnp.zeros((block, 128), jnp.float32)
        for head in range(HEADS_HERE):
            q_lanes, k_lanes, v_lanes = (
                slice(n * WIDTH + head * DH, n * WIDTH + (head + 1) * DH) for n in range(3)
            )
            q = qkv_ref[here, q_lanes]
            scores = []
            for c in range(b + 1):
                score = nt_dot(q, qkv_ref[c * block : (c + 1) * block, k_lanes]) * FACTOR
                scores.append(jnp.where(same if c < b else earlier, score, NEG))
            largest = functools.reduce(jnp.maximum, scores)
            largest = jnp.maximum(jnp.max(largest, axis=1, keepdims=True), NONE)
            weights = [jnp.exp2(score - largest) for score in scores]
            total = jnp.sum(functools.reduce(jnp.add, weights), axis=1, keepdims=True)
            out = jnp.dot(
                jnp.concatenate([w.astype(jnp.bfloat16) for w in weights], axis=1),
                qkv_ref[: (b + 1) * block, v_lanes],
                preferred_element_type=jnp.float32,
            )
            out_ref[here, head * DH : (head + 1) * DH] = out.astype(jnp.bfloat16)
            stats = stat_lanes(stats, head, largest, total)
        out_ref[here, WIDTH:] = three_parts(stats)


def col_attend(qkv):
    return pl.pallas_call(
        col_kernel,
        out_shape=jax.ShapeDtypeStruct((ROWS, WIDTH + 128), jnp.bfloat16),
        in_specs=[pl.BlockSpec(memory_space=pltpu.VMEM)],
        out_specs=pl.BlockSpec(memory_space=pltpu.VMEM),
        compiler_params=pltpu.CompilerParams(vmem_limit_bytes=VMEM),
        cost_estimate=SMALL,
        name="col_attend",
    )(qkv)


def mix_kernel(row_ref, row_stat_ref, col_ref, out_ref):
    row_max, row_total = spread_stats(row_stat_ref[...])
    col_max, col_total = spread_stats(col_ref[:, WIDTH : WIDTH + 128])
    highest = jnp.maximum(row_max, col_max)
    row_factor = jnp.exp2(row_max - highest)
    col_factor = jnp.exp2(col_max - highest)
    mixed = row_factor * row_ref[...] + col_factor * col_ref[:, :WIDTH].astype(jnp.float32)
    out_ref[...] = (mixed / (row_factor * row_total + col_factor * col_total)).astype(jnp.bfloat16)


def mix(row_out, row_stat, col):
    block = 128

    def rows(width):
        return pl.BlockSpec((block, width), lambda i: (i, 0))

    return pl.pallas_call(
        mix_kernel,
        out_shape=jax.ShapeDtypeStruct((ROWS, WIDTH), jnp.bfloat16),
        grid=(ROWS // block,),
        in_specs=[rows(WIDTH), rows(128), rows(WIDTH + 128)],
        out_specs=rows(WIDTH),
        compiler_params=pltpu.CompilerParams(vmem_limit_bytes=VMEM),
        cost_estimate=SMALL,
        name="mix",
    )(row_out, row_stat, col)


def arrange_kernel(place_ref, *refs):
    *pieces, out_ref = refs
    y, x, mp = place_ref[0], place_ref[1], place_ref[2]
    spots = []
    for i, piece in enumerate(pieces):
        there = (x + i // 2) & 3
        head = 2 * ((y + i % 2) & 1) + there // 2
        spots.append((piece, (there & 1) * 32, pl.multiple_of(head * DH, DH)))

    def step(i, carry):
        for piece, row, lane in spots:
            start = pl.multiple_of(i * 64 + row, 32)
            for group in range(N_MP):
                out_ref[group ^ mp, pl.ds(start, 32), pl.ds(lane, DH)] = piece[group, i]
        return carry

    lax.fori_loop(0, 16, step, 0)


def arrange(place, *pieces):
    vmem = pl.BlockSpec(memory_space=pltpu.VMEM)
    return pl.pallas_call(
        arrange_kernel,
        out_shape=jax.ShapeDtypeStruct((N_MP, PLANE * 32, WIDTH), jnp.bfloat16),
        in_specs=[pl.BlockSpec(memory_space=pltpu.SMEM)] + [vmem] * len(pieces),
        out_specs=vmem,
        compiler_params=pltpu.CompilerParams(vmem_limit_bytes=VMEM),
        cost_estimate=SMALL,
        name="arrange",
    )(place, *pieces)


def project_kernel(first, blocks, *refs):
    *refs, weight_ref, out_ref = refs
    step = 256
    for i in range(out_ref.shape[1] // step):
        here = slice(i * step, (i + 1) * step)
        total = refs[blocks][:, here] if len(refs) > blocks else None
        for j in range(blocks):
            term = nt_dot(refs[j][...], weight_ref[first + j, here, :])
            total = term if total is None else total + term
        out_ref[:, here] = total.astype(out_ref.dtype)


def project(before, blocks, weight, first, kind):
    operands = [*blocks] + ([] if before is None else [before]) + [weight]
    vmem = pl.BlockSpec(memory_space=pltpu.VMEM)
    return pl.pallas_call(
        functools.partial(project_kernel, first, len(blocks)),
        out_shape=jax.ShapeDtypeStruct((ROWS, PLANE * 32), kind),
        in_specs=[vmem] * len(operands),
        out_specs=vmem,
        compiler_params=pltpu.CompilerParams(vmem_limit_bytes=VMEM),
        cost_estimate=SMALL,
        name="project",
    )(*operands)


def same_parity():
    return [[i for i in range(N_SEQ) if i % 2 == p] for p in range(2)]


def swap_columns(value):
    return lax.all_to_all(
        value, "seq", split_axis=0, concat_axis=0, axis_index_groups=same_parity(), tiled=True
    )


def along(step, stride, size):
    pairs = []
    for i in range(N_SEQ):
        place = i // stride % size
        pairs.append((i, i + ((place + step) % size - place) * stride))
    return pairs


def turn(mine):
    pairs = []
    for seq in range(N_SEQ):
        z, place = divmod(seq, PLANE)
        for mp in range(N_MP):
            pairs.append((seq * N_MP + mp, (mp * PLANE + place) * N_MP + z))
    return lax.ppermute(mine, ("seq", "mp"), pairs)


def weight_messages(turned):
    heads = turned.reshape(4, 8, HEADS_HERE, DH).transpose(2, 1, 0, 3).reshape(1, 4 * 8, WIDTH)
    return jnp.broadcast_to(heads, (16, 4 * 8, WIDTH)).reshape(ROWS, WIDTH)


def weight_piece(received):
    tiles = received.reshape(64, 8, 4, DH).transpose(0, 2, 1, 3)
    return tiles.reshape(N_MP, 16, 32, DH)


def body(queries, keys, values, out_weight):
    seq, mp = lax.axis_index("seq"), lax.axis_index("mp")
    barrier = lax.optimization_barrier
    x_up, x_down = along(1, 1, 4), along(-1, 1, 4)
    y_pair = [(i, i ^ 4) for i in range(N_SEQ)]

    blank = jnp.zeros((ROWS, WIDTH), jnp.bfloat16)
    turned, together = barrier(
        (turn(out_weight.T), jnp.concatenate([queries, keys, values, blank], axis=1))
    )
    together = lax.dynamic_update_slice(together, weight_messages(turned), (0, 3 * WIDTH))
    arrived = swap_columns(together)

    to_odd = [(i, i + 1) for i in range(0, N_SEQ, 2)]
    keys_before = lax.ppermute(keys, "seq", to_odd)
    values_before = lax.ppermute(values, "seq", to_odd)

    own_0 = weight_piece(arrived[:, 3 * WIDTH :])
    own_1 = lax.ppermute(own_0, "seq", y_pair)
    less_0 = lax.ppermute(own_0, "seq", x_up)
    more_0 = lax.ppermute(own_0, "seq", x_down)

    row_out, row_stat = row_attend(
        (seq % 2).astype(jnp.int32).reshape(1), queries, keys, values, keys_before, values_before
    )
    arrived, row_out, row_stat = barrier((arrived, row_out, row_stat))

    col_own = col_attend(arrived)
    col_own, own_1, less_0, more_0 = barrier((col_own, own_1, less_0, more_0))
    less_1 = lax.ppermute(own_1, "seq", x_up)
    more_1 = lax.ppermute(own_1, "seq", x_down)
    far_0 = lax.ppermute(less_0, "seq", x_up)
    col = swap_columns(col_own)
    attended = mix(row_out, row_stat, col)

    near = [(i, i ^ 1) for i in range(N_MP)]
    far = [(i, i ^ 2) for i in range(N_MP)]
    across = lax.ppermute(attended, "mp", far)
    after, less_1, more_1 = barrier((attended, less_1, more_1))
    far_1 = lax.ppermute(more_1, "seq", x_down)
    beside = lax.ppermute(after, "mp", near)
    last = lax.ppermute(across, "mp", near)
    place = jnp.stack([seq // 4 % 8, seq % 4, mp]).astype(jnp.int32)
    weight = arrange(place, own_0, own_1, more_0, more_1, far_0, far_1, less_0, less_1)
    total = project(None, (attended, beside), weight, 0, jnp.float32)
    total = project(total, (across,), weight, 2, jnp.float32)
    return project(total, (last,), weight, 3, jnp.bfloat16)


def solution(mesh):
    placed = (P("seq", "mp"), P("seq", "mp"), P("seq", "mp"), P("mp", "seq"))
    return jax.shard_map(
        body, mesh=mesh, in_specs=placed, out_specs=P("seq", "mp"), check_vma=False
    )
```

```python
import functools

import jax
import jax.numpy as jnp
from jax import lax
from jax.experimental import pallas as pl
from jax.experimental.pallas import tpu as pltpu
from jax.sharding import PartitionSpec as P

DH = 128
HEADS_HERE = 4
ROWS = 512
WIDTH = HEADS_HERE * DH
N_MP = 4
N_SEQ = 128
PLANE = 32
COLS = 8
NEG = -1e30
NONE = -1e29
FACTOR = DH ** (-0.5) * 1.4426950408889634
VMEM = 40 * 1024 * 1024
SMALL = pl.CostEstimate(flops=1024, bytes_accessed=1024, transcendentals=0)
LARGE = pl.CostEstimate(flops=2 * 10**11, bytes_accessed=1024, transcendentals=0)

NT = (((1,), (1,)), ((), ()))


def nt_dot(a, b):
    return lax.dot_general(a, b, NT, preferred_element_type=jnp.float32)


def stat_lanes(old, head, largest, total):
    lane = lax.broadcasted_iota(jnp.int32, old.shape, 1)
    return jnp.where(lane == head, largest, jnp.where(lane == 4 + head, total, old))


def three_parts(stats):
    high = stats.astype(jnp.bfloat16).astype(jnp.float32)
    rest = stats - high
    middle = rest.astype(jnp.bfloat16).astype(jnp.float32)
    low = rest - middle
    parts = high + pltpu.roll(middle, 8, 1) + pltpu.roll(low, 16, 1)
    return parts.astype(jnp.bfloat16)


def spread_stats(stats):
    lane = lax.broadcasted_iota(jnp.int32, (128, WIDTH), 0)
    head = lax.broadcasted_iota(jnp.int32, (128, WIDTH), 1) // DH
    kept = lane < 24
    pick_max = jnp.where(kept & ((lane & 7) == head), 1.0, 0.0).astype(jnp.bfloat16)
    pick_total = jnp.where(kept & ((lane & 7) == head + 4), 1.0, 0.0).astype(jnp.bfloat16)
    largest = jnp.dot(stats, pick_max, preferred_element_type=jnp.float32)
    total = jnp.dot(stats, pick_total, preferred_element_type=jnp.float32)
    return largest, total


def row_kernel(parity_ref, q_ref, k_ref, v_ref, kp_ref, vp_ref, out_ref, packed_ref, stat_ref):
    head = pl.program_id(0)
    odd = parity_ref[0] == 1
    block = 128

    @pl.when(head == 0)
    def _():
        stat_ref[...] = jnp.zeros_like(stat_ref)

    for b in range(ROWS // block):
        here = slice(b * block, (b + 1) * block)
        seen = (b + 1) * block
        q = q_ref[here, :]
        own = nt_dot(q, k_ref[:seen, :]) * FACTOR
        place = lax.broadcasted_iota(jnp.int32, (block, seen), 0) + b * block
        other = lax.broadcasted_iota(jnp.int32, (block, seen), 1)
        own = jnp.where(other <= place, own, NEG)
        before = nt_dot(q, kp_ref[...]) * FACTOR
        before = jnp.where(odd, before, NEG)
        largest = jnp.maximum(
            jnp.max(own, axis=1, keepdims=True), jnp.max(before, axis=1, keepdims=True)
        )
        own = jnp.exp2(own - largest)
        before = jnp.exp2(before - largest)
        total = jnp.sum(own, axis=1, keepdims=True) + jnp.sum(before, axis=1, keepdims=True)
        out = jnp.dot(
            own.astype(jnp.bfloat16), v_ref[:seen, :], preferred_element_type=jnp.float32
        ) + jnp.dot(before.astype(jnp.bfloat16), vp_ref[...], preferred_element_type=jnp.float32)
        out_ref[here, :] = out.astype(jnp.bfloat16)
        stat_ref[here, :] = stat_lanes(stat_ref[here, :], head, largest, total)

    @pl.when(head == HEADS_HERE - 1)
    def _():
        packed_ref[...] = three_parts(stat_ref[...])


def row_attend(parity, q, k, v, kp, vp):
    per_head = pl.BlockSpec((ROWS, DH), lambda h, s: (0, h))
    return pl.pallas_call(
        row_kernel,
        out_shape=(
            jax.ShapeDtypeStruct((ROWS, WIDTH), jnp.bfloat16),
            jax.ShapeDtypeStruct((ROWS, 128), jnp.bfloat16),
        ),
        grid_spec=pltpu.PrefetchScalarGridSpec(
            num_scalar_prefetch=1,
            grid=(HEADS_HERE,),
            in_specs=[per_head] * 5,
            out_specs=(per_head, pl.BlockSpec((ROWS, 128), lambda h, s: (0, 0))),
            scratch_shapes=[pltpu.VMEM((ROWS, 128), jnp.float32)],
        ),
        compiler_params=pltpu.CompilerParams(vmem_limit_bytes=VMEM),
        cost_estimate=LARGE,
        name="row_attend",
    )(parity, q, k, v, kp, vp)


def col_kernel(qkv_ref, out_ref):
    block = 128
    token = lax.broadcasted_iota(jnp.int32, (block, block), 0)
    other = lax.broadcasted_iota(jnp.int32, (block, block), 1)
    same = (token & (COLS - 1)) == (other & (COLS - 1))
    earlier = same & (other < token)
    heads = range(HEADS_HERE)

    def lanes(part, head):
        return slice(part * WIDTH + head * DH, part * WIDTH + (head + 1) * DH)

    for b in range(ROWS // block):
        here = slice(b * block, (b + 1) * block)
        scores = [
            [
                jnp.where(
                    same if c < b else earlier,
                    nt_dot(
                        qkv_ref[here, lanes(0, head)],
                        qkv_ref[c * block : (c + 1) * block, lanes(1, head)],
                    )
                    * FACTOR,
                    NEG,
                )
                for c in range(b + 1)
            ]
            for head in heads
        ]
        tops = [functools.reduce(jnp.maximum, scores[head]) for head in heads]
        tops = [jnp.maximum(jnp.max(top, axis=1, keepdims=True), NONE) for top in tops]
        weights = [[jnp.exp2(score - tops[head]) for score in scores[head]] for head in heads]
        totals = [
            jnp.sum(functools.reduce(jnp.add, weights[head]), axis=1, keepdims=True)
            for head in heads
        ]
        stats = jnp.zeros((block, 128), jnp.float32)
        for head in heads:
            out = jnp.dot(
                jnp.concatenate([w.astype(jnp.bfloat16) for w in weights[head]], axis=1),
                qkv_ref[: (b + 1) * block, lanes(2, head)],
                preferred_element_type=jnp.float32,
            )
            out_ref[here, head * DH : (head + 1) * DH] = out.astype(jnp.bfloat16)
            stats = stat_lanes(stats, head, tops[head], totals[head])
        out_ref[here, WIDTH:] = three_parts(stats)


def col_attend(qkv):
    return pl.pallas_call(
        col_kernel,
        out_shape=jax.ShapeDtypeStruct((ROWS, WIDTH + 128), jnp.bfloat16),
        in_specs=[pl.BlockSpec(memory_space=pltpu.VMEM)],
        out_specs=pl.BlockSpec(memory_space=pltpu.VMEM),
        compiler_params=pltpu.CompilerParams(vmem_limit_bytes=VMEM),
        cost_estimate=LARGE,
        name="col_attend",
    )(qkv)


def mix_kernel(row_ref, row_stat_ref, col_ref, out_ref):
    row_max, row_total = spread_stats(row_stat_ref[...])
    col_max, col_total = spread_stats(col_ref[:, WIDTH : WIDTH + 128])
    highest = jnp.maximum(row_max, col_max)
    row_factor = jnp.exp2(row_max - highest)
    col_factor = jnp.exp2(col_max - highest)
    mixed = row_factor * row_ref[...].astype(jnp.float32) + col_factor * col_ref[:, :WIDTH].astype(jnp.float32)
    out_ref[...] = (mixed / (row_factor * row_total + col_factor * col_total)).astype(jnp.bfloat16)


def mix(row_out, row_stat, col):
    block = 128

    def rows(width):
        return pl.BlockSpec((block, width), lambda i: (i, 0))

    return pl.pallas_call(
        mix_kernel,
        out_shape=jax.ShapeDtypeStruct((ROWS, WIDTH), jnp.bfloat16),
        grid=(ROWS // block,),
        in_specs=[rows(WIDTH), rows(128), rows(WIDTH + 128)],
        out_specs=rows(WIDTH),
        compiler_params=pltpu.CompilerParams(vmem_limit_bytes=VMEM),
        cost_estimate=SMALL,
        name="mix",
    )(row_out, row_stat, col)


CHUNKS = 4


def finish_kernel(place_ref, *refs):
    blocks, pieces, out_ref = refs[:N_MP], refs[N_MP : N_MP + 8], refs[N_MP + 8]
    weights, results = refs[N_MP + 9 : N_MP + 9 + CHUNKS], refs[N_MP + 9 + CHUNKS : -1]
    done = refs[-1]
    y, x, mp = place_ref[0], place_ref[1], place_ref[2]
    spots = []
    for i, piece in enumerate(pieces):
        there = (x + i // 2) & 3
        head = 2 * ((y + i % 2) & 1) + there // 2
        spots.append((piece, (there & 1) * 32, pl.multiple_of(head * DH, DH)))

    copies = []
    width = PLANE * 32 // CHUNKS
    for chunk in range(CHUNKS):
        for i in range(16 // CHUNKS):
            for piece, row, lane in spots:
                start = pl.multiple_of(i * 64 + row, 32)
                for group in range(N_MP):
                    weights[chunk][group, pl.ds(start, 32), pl.ds(lane, DH)] = piece[
                        group, chunk * (16 // CHUNKS) + i
                    ]
        total = None
        for j in range(N_MP):
            term = nt_dot(blocks[j][...], weights[chunk][mp ^ j])
            total = term if total is None else total + term
        results[chunk][...] = total.astype(jnp.bfloat16)
        there = out_ref.at[:, chunk * width : (chunk + 1) * width]
        copies.append(pltpu.make_async_copy(results[chunk], there, done.at[chunk]))
        copies[-1].start()
    for copy in copies:
        copy.wait()


def finish(place, blocks, pieces):
    vmem = pl.BlockSpec(memory_space=pltpu.VMEM)
    width = PLANE * 32 // CHUNKS
    return pl.pallas_call(
        finish_kernel,
        out_shape=jax.ShapeDtypeStruct((ROWS, PLANE * 32), jnp.bfloat16),
        in_specs=[pl.BlockSpec(memory_space=pltpu.SMEM)] + [vmem] * (len(blocks) + len(pieces)),
        out_specs=pl.BlockSpec(memory_space=pl.ANY),
        scratch_shapes=[pltpu.VMEM((N_MP, width, WIDTH), jnp.bfloat16)] * CHUNKS
        + [pltpu.VMEM((ROWS, width), jnp.bfloat16)] * CHUNKS
        + [pltpu.SemaphoreType.DMA((CHUNKS,))],
        compiler_params=pltpu.CompilerParams(vmem_limit_bytes=VMEM),
        cost_estimate=SMALL,
        name="finish",
    )(place, *blocks, *pieces)


def same_parity():
    return [[i for i in range(N_SEQ) if i % 2 == p] for p in range(2)]


def swap_columns(value):
    return lax.all_to_all(
        value, "seq", split_axis=0, concat_axis=0, axis_index_groups=same_parity(), tiled=True
    )


def along(step, stride, size):
    pairs = []
    for i in range(N_SEQ):
        place = i // stride % size
        pairs.append((i, i + ((place + step) % size - place) * stride))
    return pairs


def turn(mine):
    pairs = []
    for seq in range(N_SEQ):
        z, place = divmod(seq, PLANE)
        for mp in range(N_MP):
            pairs.append((seq * N_MP + mp, (mp * PLANE + place) * N_MP + z))
    return lax.ppermute(mine, ("seq", "mp"), pairs)


def weight_messages(turned):
    heads = turned.reshape(4, 8, HEADS_HERE, DH).transpose(2, 1, 0, 3).reshape(1, 4 * 8, WIDTH)
    return jnp.broadcast_to(heads, (16, 4 * 8, WIDTH)).reshape(ROWS, WIDTH)


def weight_piece(received):
    tiles = received.reshape(64, 8, 4, DH).transpose(0, 2, 1, 3)
    return tiles.reshape(N_MP, 16, 32, DH)


def body(queries, keys, values, out_weight):
    seq, mp = lax.axis_index("seq"), lax.axis_index("mp")
    barrier = lax.optimization_barrier
    x_up, x_down = along(1, 1, 4), along(-1, 1, 4)
    y_pair = [(i, i ^ 4) for i in range(N_SEQ)]

    blank = jnp.zeros((ROWS, WIDTH), jnp.bfloat16)
    turned, together = barrier(
        (turn(out_weight.T), jnp.concatenate([queries, keys, values, blank], axis=1))
    )
    together = lax.dynamic_update_slice(together, weight_messages(turned), (0, 3 * WIDTH))
    arrived = swap_columns(together)

    to_odd = [(i, i + 1) for i in range(0, N_SEQ, 2)]
    keys_before = lax.ppermute(keys, "seq", to_odd)
    values_before = lax.ppermute(values, "seq", to_odd)

    own_0 = weight_piece(arrived[:, 3 * WIDTH :])
    own_1 = lax.ppermute(own_0, "seq", y_pair)
    less_0 = lax.ppermute(own_0, "seq", x_up)
    more_0 = lax.ppermute(own_0, "seq", x_down)

    col_own = col_attend(arrived)
    col_own, keys_before, values_before = barrier((col_own, keys_before, values_before))
    keys_before, values_before, own_1, less_0, more_0 = barrier(
        (keys_before, values_before, own_1, less_0, more_0)
    )
    row_out, row_stat = row_attend(
        (seq % 2).astype(jnp.int32).reshape(1), queries, keys, values, keys_before, values_before
    )
    less_1 = lax.ppermute(own_1, "seq", x_up)
    more_1 = lax.ppermute(own_1, "seq", x_down)
    far_0 = lax.ppermute(less_0, "seq", x_up)
    col = swap_columns(col_own)
    attended = mix(row_out, row_stat, col)

    near = [(i, i ^ 1) for i in range(N_MP)]
    far = [(i, i ^ 2) for i in range(N_MP)]
    across = lax.ppermute(attended, "mp", far)
    after, less_1, more_1 = barrier((attended, less_1, more_1))
    far_1 = lax.ppermute(more_1, "seq", x_down)
    after, across = barrier((after, across))
    beside = lax.ppermute(after, "mp", near)
    last = lax.ppermute(across, "mp", near)
    place = jnp.stack([seq // 4 % 8, seq % 4, mp]).astype(jnp.int32)
    pieces = (own_0, own_1, more_0, more_1, far_0, far_1, less_0, less_1)
    return finish(place, (after, beside, across, last), pieces)


def solution(mesh):
    placed = (P("seq", "mp"), P("seq", "mp"), P("seq", "mp"), P("mp", "seq"))
    return jax.shard_map(
        body, mesh=mesh, in_specs=placed, out_specs=P("seq", "mp"), check_vma=False
    )
```

```python
import functools

import jax
import jax.numpy as jnp
from jax import lax
from jax.experimental import pallas as pl
from jax.experimental.pallas import tpu as pltpu
from jax.sharding import PartitionSpec as P

DH = 128
HEADS_HERE = 4
ROWS = 512
WIDTH = HEADS_HERE * DH
N_MP = 4
N_SEQ = 128
PLANE = 32
COLS = 8
NEG = -1e30
NONE = -1e29
FACTOR = DH ** (-0.5) * 1.4426950408889634
VMEM = 40 * 1024 * 1024
SMALL = pl.CostEstimate(flops=1024, bytes_accessed=1024, transcendentals=0)
LARGE = pl.CostEstimate(flops=2 * 10**11, bytes_accessed=1024, transcendentals=0)

NT = (((1,), (1,)), ((), ()))


def nt_dot(a, b):
    return lax.dot_general(a, b, NT, preferred_element_type=jnp.float32)


def stat_lanes(old, head, largest, total):
    lane = lax.broadcasted_iota(jnp.int32, old.shape, 1)
    return jnp.where(lane == head, largest, jnp.where(lane == 4 + head, total, old))


def three_parts(stats):
    high = stats.astype(jnp.bfloat16).astype(jnp.float32)
    rest = stats - high
    middle = rest.astype(jnp.bfloat16).astype(jnp.float32)
    low = rest - middle
    parts = high + pltpu.roll(middle, 8, 1) + pltpu.roll(low, 16, 1)
    return parts.astype(jnp.bfloat16)


def spread_stats(stats):
    lane = lax.broadcasted_iota(jnp.int32, (128, WIDTH), 0)
    head = lax.broadcasted_iota(jnp.int32, (128, WIDTH), 1) // DH
    kept = lane < 24
    pick_max = jnp.where(kept & ((lane & 7) == head), 1.0, 0.0).astype(jnp.bfloat16)
    pick_total = jnp.where(kept & ((lane & 7) == head + 4), 1.0, 0.0).astype(jnp.bfloat16)
    largest = jnp.dot(stats, pick_max, preferred_element_type=jnp.float32)
    total = jnp.dot(stats, pick_total, preferred_element_type=jnp.float32)
    return largest, total


def head_lanes(head, part=0):
    return slice(part * WIDTH + head * DH, part * WIDTH + (head + 1) * DH)


def soften(scores):
    top = jnp.max(functools.reduce(jnp.maximum, scores), axis=1, keepdims=True)
    top = jnp.maximum(top, NONE)
    weights = [jnp.exp2(score - top) for score in scores]
    total = jnp.sum(functools.reduce(jnp.add, weights), axis=1, keepdims=True)
    return top, weights, total


def row_kernel(parity_ref, q_ref, k_ref, v_ref, kp_ref, vp_ref, out_ref, packed_ref):
    odd = parity_ref[0] == 1
    block = 128
    token = lax.broadcasted_iota(jnp.int32, (block, block), 0)
    other = lax.broadcasted_iota(jnp.int32, (block, block), 1)
    causal = other <= token
    heads = range(HEADS_HERE)
    for b in range(ROWS // block):
        here = slice(b * block, (b + 1) * block)
        scores = []
        for head in heads:
            lanes = head_lanes(head)
            q = q_ref[here, lanes]
            row = []
            for c in range(b + 1):
                score = nt_dot(q, k_ref[c * block : (c + 1) * block, lanes]) * FACTOR
                row.append(score if c < b else jnp.where(causal, score, NEG))
            for c in range(ROWS // block):
                score = nt_dot(q, kp_ref[c * block : (c + 1) * block, lanes]) * FACTOR
                row.append(jnp.where(odd, score, NEG))
            scores.append(row)
        soft = [soften(row) for row in scores]
        stats = jnp.zeros((block, 128), jnp.float32)
        for head in heads:
            lanes = head_lanes(head)
            top, weights, total = soft[head]
            weights = [w.astype(jnp.bfloat16) for w in weights]
            out = jnp.dot(
                jnp.concatenate(weights[: b + 1], axis=1),
                v_ref[: (b + 1) * block, lanes],
                preferred_element_type=jnp.float32,
            ) + jnp.dot(
                jnp.concatenate(weights[b + 1 :], axis=1),
                vp_ref[:, lanes],
                preferred_element_type=jnp.float32,
            )
            out_ref[here, lanes] = out.astype(jnp.bfloat16)
            stats = stat_lanes(stats, head, top, total)
        packed_ref[here, :] = three_parts(stats)


def row_attend(parity, q, k, v, kp, vp):
    vmem = pl.BlockSpec(memory_space=pltpu.VMEM)
    return pl.pallas_call(
        row_kernel,
        out_shape=(
            jax.ShapeDtypeStruct((ROWS, WIDTH), jnp.bfloat16),
            jax.ShapeDtypeStruct((ROWS, 128), jnp.bfloat16),
        ),
        in_specs=[pl.BlockSpec(memory_space=pltpu.SMEM)] + [vmem] * 5,
        out_specs=(vmem, vmem),
        compiler_params=pltpu.CompilerParams(vmem_limit_bytes=VMEM),
        cost_estimate=LARGE,
        name="row_attend",
    )(parity, q, k, v, kp, vp)


def col_kernel(qkv_ref, out_ref):
    block = 128
    token = lax.broadcasted_iota(jnp.int32, (block, block), 0)
    other = lax.broadcasted_iota(jnp.int32, (block, block), 1)
    same = (token & (COLS - 1)) == (other & (COLS - 1))
    earlier = same & (other < token)
    heads = range(HEADS_HERE)

    def lanes(part, head):
        return slice(part * WIDTH + head * DH, part * WIDTH + (head + 1) * DH)

    for b in range(ROWS // block):
        here = slice(b * block, (b + 1) * block)
        scores = [
            [
                jnp.where(
                    same if c < b else earlier,
                    nt_dot(
                        qkv_ref[here, lanes(0, head)],
                        qkv_ref[c * block : (c + 1) * block, lanes(1, head)],
                    )
                    * FACTOR,
                    NEG,
                )
                for c in range(b + 1)
            ]
            for head in heads
        ]
        tops = [functools.reduce(jnp.maximum, scores[head]) for head in heads]
        tops = [jnp.maximum(jnp.max(top, axis=1, keepdims=True), NONE) for top in tops]
        weights = [[jnp.exp2(score - tops[head]) for score in scores[head]] for head in heads]
        totals = [
            jnp.sum(functools.reduce(jnp.add, weights[head]), axis=1, keepdims=True)
            for head in heads
        ]
        stats = jnp.zeros((block, 128), jnp.float32)
        for head in heads:
            out = jnp.dot(
                jnp.concatenate([w.astype(jnp.bfloat16) for w in weights[head]], axis=1),
                qkv_ref[: (b + 1) * block, lanes(2, head)],
                preferred_element_type=jnp.float32,
            )
            out_ref[here, head * DH : (head + 1) * DH] = out.astype(jnp.bfloat16)
            stats = stat_lanes(stats, head, tops[head], totals[head])
        out_ref[here, WIDTH:] = three_parts(stats)


def col_attend(qkv):
    return pl.pallas_call(
        col_kernel,
        out_shape=jax.ShapeDtypeStruct((ROWS, WIDTH + 128), jnp.bfloat16),
        in_specs=[pl.BlockSpec(memory_space=pltpu.VMEM)],
        out_specs=pl.BlockSpec(memory_space=pltpu.VMEM),
        compiler_params=pltpu.CompilerParams(vmem_limit_bytes=VMEM),
        cost_estimate=LARGE,
        name="col_attend",
    )(qkv)


def mix_kernel(row_ref, row_stat_ref, col_ref, out_ref):
    block = 128
    for b in range(ROWS // block):
        here = slice(b * block, (b + 1) * block)
        row_max, row_total = spread_stats(row_stat_ref[here, :])
        col_max, col_total = spread_stats(col_ref[here, WIDTH : WIDTH + 128])
        highest = jnp.maximum(row_max, col_max)
        row_factor = jnp.exp2(row_max - highest)
        col_factor = jnp.exp2(col_max - highest)
        row, col = (ref[here, :WIDTH].astype(jnp.float32) for ref in (row_ref, col_ref))
        mixed = row_factor * row + col_factor * col
        total = row_factor * row_total + col_factor * col_total
        out_ref[here, :] = (mixed / total).astype(jnp.bfloat16)


def mix(row_out, row_stat, col):
    vmem = pl.BlockSpec(memory_space=pltpu.VMEM)
    return pl.pallas_call(
        mix_kernel,
        out_shape=jax.ShapeDtypeStruct((ROWS, WIDTH), jnp.bfloat16),
        in_specs=[vmem] * 3,
        out_specs=vmem,
        compiler_params=pltpu.CompilerParams(vmem_limit_bytes=VMEM),
        cost_estimate=SMALL,
        name="mix",
    )(row_out, row_stat, col)


CHUNKS = 4


def finish_kernel(place_ref, *refs):
    blocks, pieces, out_ref = refs[:N_MP], refs[N_MP : N_MP + 8], refs[N_MP + 8]
    weights, results = refs[N_MP + 9 : N_MP + 9 + CHUNKS], refs[N_MP + 9 + CHUNKS : -1]
    done = refs[-1]
    y, x, mp = place_ref[0], place_ref[1], place_ref[2]
    spots = []
    for i, piece in enumerate(pieces):
        there = (x + i // 2) & 3
        head = 2 * ((y + i % 2) & 1) + there // 2
        spots.append((piece, (there & 1) * 32, pl.multiple_of(head * DH, DH)))

    copies = []
    width = PLANE * 32 // CHUNKS
    for chunk in range(CHUNKS):
        for i in range(16 // CHUNKS):
            for piece, row, lane in spots:
                start = pl.multiple_of(i * 64 + row, 32)
                for group in range(N_MP):
                    weights[chunk][group, pl.ds(start, 32), pl.ds(lane, DH)] = piece[
                        group, chunk * (16 // CHUNKS) + i
                    ]
        total = None
        for j in range(N_MP):
            term = nt_dot(blocks[j][...], weights[chunk][mp ^ j])
            total = term if total is None else total + term
        results[chunk][...] = total.astype(jnp.bfloat16)
        there = out_ref.at[:, chunk * width : (chunk + 1) * width]
        copies.append(pltpu.make_async_copy(results[chunk], there, done.at[chunk]))
        copies[-1].start()
    for copy in copies:
        copy.wait()


def finish(place, blocks, pieces):
    vmem = pl.BlockSpec(memory_space=pltpu.VMEM)
    width = PLANE * 32 // CHUNKS
    return pl.pallas_call(
        finish_kernel,
        out_shape=jax.ShapeDtypeStruct((ROWS, PLANE * 32), jnp.bfloat16),
        in_specs=[pl.BlockSpec(memory_space=pltpu.SMEM)] + [vmem] * (len(blocks) + len(pieces)),
        out_specs=pl.BlockSpec(memory_space=pl.ANY),
        scratch_shapes=[pltpu.VMEM((N_MP, width, WIDTH), jnp.bfloat16)] * CHUNKS
        + [pltpu.VMEM((ROWS, width), jnp.bfloat16)] * CHUNKS
        + [pltpu.SemaphoreType.DMA((CHUNKS,))],
        compiler_params=pltpu.CompilerParams(vmem_limit_bytes=VMEM),
        cost_estimate=SMALL,
        name="finish",
    )(place, *blocks, *pieces)


def same_parity():
    return [[i for i in range(N_SEQ) if i % 2 == p] for p in range(2)]


def swap_columns(value):
    return lax.all_to_all(
        value, "seq", split_axis=0, concat_axis=0, axis_index_groups=same_parity(), tiled=True
    )


def along(step, stride, size):
    pairs = []
    for i in range(N_SEQ):
        place = i // stride % size
        pairs.append((i, i + ((place + step) % size - place) * stride))
    return pairs


def turn(mine):
    pairs = []
    for seq in range(N_SEQ):
        z, place = divmod(seq, PLANE)
        for mp in range(N_MP):
            pairs.append((seq * N_MP + mp, (mp * PLANE + place) * N_MP + z))
    return lax.ppermute(mine, ("seq", "mp"), pairs)


def weight_messages(turned):
    heads = turned.reshape(4, 8, HEADS_HERE, DH).transpose(2, 1, 0, 3).reshape(1, 4 * 8, WIDTH)
    return jnp.broadcast_to(heads, (16, 4 * 8, WIDTH)).reshape(ROWS, WIDTH)


def weight_piece(received):
    tiles = received.reshape(64, 8, 4, DH).transpose(0, 2, 1, 3)
    return tiles.reshape(N_MP, 16, 32, DH)


def body(queries, keys, values, out_weight):
    seq, mp = lax.axis_index("seq"), lax.axis_index("mp")
    barrier = lax.optimization_barrier
    x_up, x_down = along(1, 1, 4), along(-1, 1, 4)
    y_pair = [(i, i ^ 4) for i in range(N_SEQ)]

    blank = jnp.zeros((ROWS, WIDTH), jnp.bfloat16)
    turned, together = barrier(
        (turn(out_weight.T), jnp.concatenate([queries, keys, values, blank], axis=1))
    )
    together = lax.dynamic_update_slice(together, weight_messages(turned), (0, 3 * WIDTH))
    arrived = swap_columns(together)

    to_odd = [(i, i + 1) for i in range(0, N_SEQ, 2)]
    keys_before = lax.ppermute(keys, "seq", to_odd)
    values_before = lax.ppermute(values, "seq", to_odd)

    own_0 = weight_piece(arrived[:, 3 * WIDTH :])
    own_1 = lax.ppermute(own_0, "seq", y_pair)

    col_own = col_attend(arrived)
    col_own, keys_before, values_before, own_0 = barrier(
        (col_own, keys_before, values_before, own_0)
    )
    keys_before, values_before, own_1 = barrier((keys_before, values_before, own_1))
    less_0 = lax.ppermute(own_0, "seq", x_up)
    more_0 = lax.ppermute(own_0, "seq", x_down)
    row_out, row_stat = row_attend(
        (seq % 2).astype(jnp.int32).reshape(1), queries, keys, values, keys_before, values_before
    )
    less_1 = lax.ppermute(own_1, "seq", x_up)
    more_1 = lax.ppermute(own_1, "seq", x_down)
    col = swap_columns(col_own)
    attended = mix(row_out, row_stat, col)

    near = [(i, i ^ 1) for i in range(N_MP)]
    far = [(i, i ^ 2) for i in range(N_MP)]
    across = lax.ppermute(attended, "mp", far)
    after, less_0, more_0, less_1, more_1 = barrier((attended, less_0, more_0, less_1, more_1))
    far_0 = lax.ppermute(less_0, "seq", x_up)
    far_1 = lax.ppermute(more_1, "seq", x_down)
    after, across = barrier((after, across))
    beside = lax.ppermute(after, "mp", near)
    last = lax.ppermute(across, "mp", near)
    place = jnp.stack([seq // 4 % 8, seq % 4, mp]).astype(jnp.int32)
    pieces = (own_0, own_1, more_0, more_1, far_0, far_1, less_0, less_1)
    return finish(place, (after, beside, across, last), pieces)


def solution(mesh):
    placed = (P("seq", "mp"), P("seq", "mp"), P("seq", "mp"), P("mp", "seq"))
    return jax.shard_map(
        body, mesh=mesh, in_specs=placed, out_specs=P("seq", "mp"), check_vma=False
    )
```

```python
import functools

import jax
import jax.numpy as jnp
from jax import lax
from jax.experimental import pallas as pl
from jax.experimental.pallas import tpu as pltpu
from jax.sharding import PartitionSpec as P

DH = 128
HEADS_HERE = 4
ROWS = 512
WIDTH = HEADS_HERE * DH
N_MP = 4
N_SEQ = 128
PLANE = 32
COLS = 8
NEG = -1e30
NONE = -1e29
FACTOR = DH ** (-0.5) * 1.4426950408889634
VMEM = 40 * 1024 * 1024
SMALL = pl.CostEstimate(flops=1024, bytes_accessed=1024, transcendentals=0)
LARGE = pl.CostEstimate(flops=2 * 10**11, bytes_accessed=1024, transcendentals=0)

NT = (((1,), (1,)), ((), ()))


def nt_dot(a, b):
    return lax.dot_general(a, b, NT, preferred_element_type=jnp.float32)


def stat_lanes(old, head, largest, total):
    lane = lax.broadcasted_iota(jnp.int32, old.shape, 1)
    return jnp.where(lane == head, largest, jnp.where(lane == 4 + head, total, old))


def three_parts(stats):
    high = stats.astype(jnp.bfloat16).astype(jnp.float32)
    rest = stats - high
    middle = rest.astype(jnp.bfloat16).astype(jnp.float32)
    low = rest - middle
    parts = high + pltpu.roll(middle, 8, 1) + pltpu.roll(low, 16, 1)
    return parts.astype(jnp.bfloat16)


def spread_stats(stats):
    lane = lax.broadcasted_iota(jnp.int32, (128, WIDTH), 0)
    head = lax.broadcasted_iota(jnp.int32, (128, WIDTH), 1) // DH
    kept = lane < 24
    pick_max = jnp.where(kept & ((lane & 7) == head), 1.0, 0.0).astype(jnp.bfloat16)
    pick_total = jnp.where(kept & ((lane & 7) == head + 4), 1.0, 0.0).astype(jnp.bfloat16)
    largest = jnp.dot(stats, pick_max, preferred_element_type=jnp.float32)
    total = jnp.dot(stats, pick_total, preferred_element_type=jnp.float32)
    return largest, total


def head_lanes(head, part=0):
    return slice(part * WIDTH + head * DH, part * WIDTH + (head + 1) * DH)


def soften(scores):
    top = jnp.max(functools.reduce(jnp.maximum, scores), axis=1, keepdims=True)
    top = jnp.maximum(top, NONE)
    weights = [jnp.exp2(score - top) for score in scores]
    total = jnp.sum(functools.reduce(jnp.add, weights), axis=1, keepdims=True)
    return top, weights, total


def row_kernel(parity_ref, q_ref, k_ref, v_ref, kp_ref, vp_ref, out_ref, packed_ref):
    odd = parity_ref[0] == 1
    block = 128
    token = lax.broadcasted_iota(jnp.int32, (block, block), 0)
    other = lax.broadcasted_iota(jnp.int32, (block, block), 1)
    causal = other <= token
    heads = range(HEADS_HERE)
    for b in range(ROWS // block):
        here = slice(b * block, (b + 1) * block)
        scores = []
        for head in heads:
            lanes = head_lanes(head)
            q = q_ref[here, lanes]
            row = []
            for c in range(b + 1):
                score = nt_dot(q, k_ref[c * block : (c + 1) * block, lanes]) * FACTOR
                row.append(score if c < b else jnp.where(causal, score, NEG))
            for c in range(ROWS // block):
                score = nt_dot(q, kp_ref[c * block : (c + 1) * block, lanes]) * FACTOR
                row.append(jnp.where(odd, score, NEG))
            scores.append(row)
        soft = [soften(row) for row in scores]
        stats = jnp.zeros((block, 128), jnp.float32)
        for head in heads:
            lanes = head_lanes(head)
            top, weights, total = soft[head]
            weights = [w.astype(jnp.bfloat16) for w in weights]
            out = jnp.dot(
                jnp.concatenate(weights[: b + 1], axis=1),
                v_ref[: (b + 1) * block, lanes],
                preferred_element_type=jnp.float32,
            ) + jnp.dot(
                jnp.concatenate(weights[b + 1 :], axis=1),
                vp_ref[:, lanes],
                preferred_element_type=jnp.float32,
            )
            out_ref[here, lanes] = out.astype(jnp.bfloat16)
            stats = stat_lanes(stats, head, top, total)
        packed_ref[here, :] = three_parts(stats)


def row_attend(parity, q, k, v, kp, vp):
    vmem = pl.BlockSpec(memory_space=pltpu.VMEM)
    return pl.pallas_call(
        row_kernel,
        out_shape=(
            jax.ShapeDtypeStruct((ROWS, WIDTH), jnp.bfloat16),
            jax.ShapeDtypeStruct((ROWS, 128), jnp.bfloat16),
        ),
        in_specs=[pl.BlockSpec(memory_space=pltpu.SMEM)] + [vmem] * 5,
        out_specs=(vmem, vmem),
        compiler_params=pltpu.CompilerParams(vmem_limit_bytes=VMEM),
        cost_estimate=LARGE,
        name="row_attend",
    )(parity, q, k, v, kp, vp)


def col_kernel(qkv_ref, out_ref):
    block = 128
    token = lax.broadcasted_iota(jnp.int32, (block, block), 0)
    other = lax.broadcasted_iota(jnp.int32, (block, block), 1)
    same = (token & (COLS - 1)) == (other & (COLS - 1))
    earlier = same & (other < token)
    heads = range(HEADS_HERE)

    def lanes(part, head):
        return slice(part * WIDTH + head * DH, part * WIDTH + (head + 1) * DH)

    for b in range(ROWS // block):
        here = slice(b * block, (b + 1) * block)
        scores = [
            [
                jnp.where(
                    same if c < b else earlier,
                    nt_dot(
                        qkv_ref[here, lanes(0, head)],
                        qkv_ref[c * block : (c + 1) * block, lanes(1, head)],
                    )
                    * FACTOR,
                    NEG,
                )
                for c in range(b + 1)
            ]
            for head in heads
        ]
        tops = [functools.reduce(jnp.maximum, scores[head]) for head in heads]
        tops = [jnp.maximum(jnp.max(top, axis=1, keepdims=True), NONE) for top in tops]
        weights = [[jnp.exp2(score - tops[head]) for score in scores[head]] for head in heads]
        totals = [
            jnp.sum(functools.reduce(jnp.add, weights[head]), axis=1, keepdims=True)
            for head in heads
        ]
        stats = jnp.zeros((block, 128), jnp.float32)
        for head in heads:
            out = jnp.dot(
                jnp.concatenate([w.astype(jnp.bfloat16) for w in weights[head]], axis=1),
                qkv_ref[: (b + 1) * block, lanes(2, head)],
                preferred_element_type=jnp.float32,
            )
            out_ref[here, head * DH : (head + 1) * DH] = out.astype(jnp.bfloat16)
            stats = stat_lanes(stats, head, tops[head], totals[head])
        out_ref[here, WIDTH:] = three_parts(stats)


def col_attend(qkv):
    return pl.pallas_call(
        col_kernel,
        out_shape=jax.ShapeDtypeStruct((ROWS, WIDTH + 128), jnp.bfloat16),
        in_specs=[pl.BlockSpec(memory_space=pltpu.VMEM)],
        out_specs=pl.BlockSpec(memory_space=pltpu.VMEM),
        compiler_params=pltpu.CompilerParams(vmem_limit_bytes=VMEM),
        cost_estimate=LARGE,
        name="col_attend",
    )(qkv)


def mix_kernel(row_ref, row_stat_ref, col_ref, out_ref):
    block = 128
    for b in range(ROWS // block):
        here = slice(b * block, (b + 1) * block)
        row_max, row_total = spread_stats(row_stat_ref[here, :])
        col_max, col_total = spread_stats(col_ref[here, WIDTH : WIDTH + 128])
        highest = jnp.maximum(row_max, col_max)
        row_factor = jnp.exp2(row_max - highest)
        col_factor = jnp.exp2(col_max - highest)
        row, col = (ref[here, :WIDTH].astype(jnp.float32) for ref in (row_ref, col_ref))
        mixed = row_factor * row + col_factor * col
        total = row_factor * row_total + col_factor * col_total
        out_ref[here, :] = (mixed / total).astype(jnp.bfloat16)


def mix(row_out, row_stat, col):
    vmem = pl.BlockSpec(memory_space=pltpu.VMEM)
    return pl.pallas_call(
        mix_kernel,
        out_shape=jax.ShapeDtypeStruct((ROWS, WIDTH), jnp.bfloat16),
        in_specs=[vmem] * 3,
        out_specs=vmem,
        compiler_params=pltpu.CompilerParams(vmem_limit_bytes=VMEM),
        cost_estimate=SMALL,
        name="mix",
    )(row_out, row_stat, col)


CHUNKS = 4
EARLY = ((0, 0), (0, 1), (1, 0), (1, 1), (3, 0), (3, 1))
LATE = ((2, 0), (2, 1))


def put_pieces(place_ref, pieces, origins, weight_ref, places):
    y, x, mp = place_ref[0], place_ref[1], place_ref[2]
    for (step, other), piece in zip(origins, pieces):
        there = (x + step) & 3
        lane = pl.multiple_of((2 * ((y + other) & 1) + there // 2) * DH, DH)
        for i in places:
            start = pl.multiple_of(i * 64 + (there & 1) * 32, 32)
            for group in range(N_MP):
                weight_ref[group ^ mp, pl.ds(start, 32), pl.ds(lane, DH)] = piece[group, i]


def arrange_kernel(place_ref, *refs):
    put_pieces(place_ref, refs[:-1], EARLY, refs[-1], range(16))


def arrange(place, pieces):
    vmem = pl.BlockSpec(memory_space=pltpu.VMEM)
    return pl.pallas_call(
        arrange_kernel,
        out_shape=jax.ShapeDtypeStruct((N_MP, PLANE * 32, WIDTH), jnp.bfloat16),
        in_specs=[pl.BlockSpec(memory_space=pltpu.SMEM)] + [vmem] * len(pieces),
        out_specs=vmem,
        compiler_params=pltpu.CompilerParams(vmem_limit_bytes=VMEM),
        cost_estimate=SMALL,
        name="arrange",
    )(place, *pieces)


def finish_kernel(place_ref, *refs):
    blocks, pieces = refs[:N_MP], refs[N_MP : N_MP + 2]
    out_ref, weight_ref, *results, done = refs[N_MP + 3 :]
    copies = []
    width = PLANE * 32 // CHUNKS
    for chunk in range(CHUNKS):
        here = slice(chunk * width, (chunk + 1) * width)
        part = 16 // CHUNKS
        put_pieces(place_ref, pieces, LATE, weight_ref, range(chunk * part, (chunk + 1) * part))
        total = None
        for j in range(N_MP):
            term = nt_dot(blocks[j][...], weight_ref[j, here, :])
            total = term if total is None else total + term
        results[chunk][...] = total.astype(jnp.bfloat16)
        copies.append(
            pltpu.make_async_copy(results[chunk], out_ref.at[:, here], done.at[chunk])
        )
        copies[-1].start()
    for copy in copies:
        copy.wait()


def finish(place, blocks, pieces, weight):
    vmem = pl.BlockSpec(memory_space=pltpu.VMEM)
    width = PLANE * 32 // CHUNKS
    inputs = (*blocks, *pieces, weight)
    return pl.pallas_call(
        finish_kernel,
        out_shape=(
            jax.ShapeDtypeStruct((ROWS, PLANE * 32), jnp.bfloat16),
            jax.ShapeDtypeStruct(weight.shape, weight.dtype),
        ),
        in_specs=[pl.BlockSpec(memory_space=pltpu.SMEM)] + [vmem] * len(inputs),
        out_specs=(pl.BlockSpec(memory_space=pl.ANY), vmem),
        input_output_aliases={len(inputs): 1},
        scratch_shapes=[pltpu.VMEM((ROWS, width), jnp.bfloat16)] * CHUNKS
        + [pltpu.SemaphoreType.DMA((CHUNKS,))],
        compiler_params=pltpu.CompilerParams(vmem_limit_bytes=VMEM),
        cost_estimate=SMALL,
        name="finish",
    )(place, *inputs)[0]


def same_parity():
    return [[i for i in range(N_SEQ) if i % 2 == p] for p in range(2)]


def swap_columns(value):
    return lax.all_to_all(
        value, "seq", split_axis=0, concat_axis=0, axis_index_groups=same_parity(), tiled=True
    )


def along(step, stride, size):
    pairs = []
    for i in range(N_SEQ):
        place = i // stride % size
        pairs.append((i, i + ((place + step) % size - place) * stride))
    return pairs


def turn(mine):
    pairs = []
    for seq in range(N_SEQ):
        z, place = divmod(seq, PLANE)
        for mp in range(N_MP):
            pairs.append((seq * N_MP + mp, (mp * PLANE + place) * N_MP + z))
    return lax.ppermute(mine, ("seq", "mp"), pairs)


def weight_messages(turned):
    heads = turned.reshape(4, 8, HEADS_HERE, DH).transpose(2, 1, 0, 3).reshape(1, 4 * 8, WIDTH)
    return jnp.broadcast_to(heads, (16, 4 * 8, WIDTH)).reshape(ROWS, WIDTH)


def weight_piece(received):
    tiles = received.reshape(64, 8, 4, DH).transpose(0, 2, 1, 3)
    return tiles.reshape(N_MP, 16, 32, DH)


def body(queries, keys, values, out_weight):
    seq, mp = lax.axis_index("seq"), lax.axis_index("mp")
    barrier = lax.optimization_barrier
    x_up, x_down = along(1, 1, 4), along(-1, 1, 4)
    y_pair = [(i, i ^ 4) for i in range(N_SEQ)]

    blank = jnp.zeros((ROWS, WIDTH), jnp.bfloat16)
    turned, together = barrier(
        (turn(out_weight.T), jnp.concatenate([queries, keys, values, blank], axis=1))
    )
    together = lax.dynamic_update_slice(together, weight_messages(turned), (0, 3 * WIDTH))
    arrived = swap_columns(together)

    to_odd = [(i, i + 1) for i in range(0, N_SEQ, 2)]
    keys_before = lax.ppermute(keys, "seq", to_odd)
    values_before = lax.ppermute(values, "seq", to_odd)

    own_0 = weight_piece(arrived[:, 3 * WIDTH :])
    own_1 = lax.ppermute(own_0, "seq", y_pair)

    col_own = col_attend(arrived)
    col_own, keys_before, values_before, own_0 = barrier(
        (col_own, keys_before, values_before, own_0)
    )
    keys_before, values_before, own_1 = barrier((keys_before, values_before, own_1))
    less_0 = lax.ppermute(own_0, "seq", x_up)
    more_0 = lax.ppermute(own_0, "seq", x_down)
    row_out, row_stat = row_attend(
        (seq % 2).astype(jnp.int32).reshape(1), queries, keys, values, keys_before, values_before
    )
    less_1 = lax.ppermute(own_1, "seq", x_up)
    more_1 = lax.ppermute(own_1, "seq", x_down)
    col = swap_columns(col_own)
    attended = mix(row_out, row_stat, col)

    near = [(i, i ^ 1) for i in range(N_MP)]
    far = [(i, i ^ 2) for i in range(N_MP)]
    across = lax.ppermute(attended, "mp", far)
    after, less_0, more_0, less_1, more_1 = barrier((attended, less_0, more_0, less_1, more_1))
    far_0 = lax.ppermute(less_0, "seq", x_up)
    far_1 = lax.ppermute(more_1, "seq", x_down)
    place = jnp.stack([seq // 4 % 8, seq % 4, mp]).astype(jnp.int32)
    weight = arrange(place, (own_0, own_1, more_0, more_1, less_0, less_1))
    after, weight = barrier((after, weight))
    beside = lax.ppermute(after, "mp", near)
    last = lax.ppermute(across, "mp", near)
    return finish(place, (after, beside, across, last), (far_0, far_1), weight)


def solution(mesh):
    placed = (P("seq", "mp"), P("seq", "mp"), P("seq", "mp"), P("mp", "seq"))
    return jax.shard_map(
        body, mesh=mesh, in_specs=placed, out_specs=P("seq", "mp"), check_vma=False
    )
```

```python
import functools

import jax
import jax.numpy as jnp
from jax import lax
from jax.experimental import pallas as pl
from jax.experimental.pallas import tpu as pltpu
from jax.sharding import PartitionSpec as P

DH = 128
HEADS_HERE = 4
ROWS = 512
WIDTH = HEADS_HERE * DH
N_MP = 4
N_SEQ = 128
PLANE = 32
COLS = 8
NEG = -1e30
NONE = -1e29
FACTOR = DH ** (-0.5) * 1.4426950408889634
VMEM = 40 * 1024 * 1024
SMALL = pl.CostEstimate(flops=1024, bytes_accessed=1024, transcendentals=0)
LARGE = pl.CostEstimate(flops=2 * 10**11, bytes_accessed=1024, transcendentals=0)

NT = (((1,), (1,)), ((), ()))


def nt_dot(a, b):
    return lax.dot_general(a, b, NT, preferred_element_type=jnp.float32)


def stat_lanes(old, head, largest, total):
    lane = lax.broadcasted_iota(jnp.int32, old.shape, 1)
    return jnp.where(lane == head, largest, jnp.where(lane == 4 + head, total, old))


def three_parts(stats):
    high = stats.astype(jnp.bfloat16).astype(jnp.float32)
    rest = stats - high
    middle = rest.astype(jnp.bfloat16).astype(jnp.float32)
    low = rest - middle
    parts = high + pltpu.roll(middle, 8, 1) + pltpu.roll(low, 16, 1)
    return parts.astype(jnp.bfloat16)


def spread_stats(stats):
    lane = lax.broadcasted_iota(jnp.int32, (128, WIDTH), 0)
    head = lax.broadcasted_iota(jnp.int32, (128, WIDTH), 1) // DH
    kept = lane < 24
    pick_max = jnp.where(kept & ((lane & 7) == head), 1.0, 0.0).astype(jnp.bfloat16)
    pick_total = jnp.where(kept & ((lane & 7) == head + 4), 1.0, 0.0).astype(jnp.bfloat16)
    largest = jnp.dot(stats, pick_max, preferred_element_type=jnp.float32)
    total = jnp.dot(stats, pick_total, preferred_element_type=jnp.float32)
    return largest, total


def head_lanes(head, part=0):
    return slice(part * WIDTH + head * DH, part * WIDTH + (head + 1) * DH)


def soften(scores):
    top = jnp.max(functools.reduce(jnp.maximum, scores), axis=1, keepdims=True)
    top = jnp.maximum(top, NONE)
    weights = [jnp.exp2(score - top) for score in scores]
    total = jnp.sum(functools.reduce(jnp.add, weights), axis=1, keepdims=True)
    return top, weights, total


def row_kernel(parity_ref, q_ref, k_ref, v_ref, kp_ref, vp_ref, out_ref, packed_ref):
    odd = parity_ref[0] == 1
    block = 128
    token = lax.broadcasted_iota(jnp.int32, (block, block), 0)
    other = lax.broadcasted_iota(jnp.int32, (block, block), 1)
    causal = other <= token
    heads = range(HEADS_HERE)
    for b in range(ROWS // block):
        here = slice(b * block, (b + 1) * block)
        scores = []
        for head in heads:
            lanes = head_lanes(head)
            q = q_ref[here, lanes]
            row = []
            for c in range(b + 1):
                score = nt_dot(q, k_ref[c * block : (c + 1) * block, lanes]) * FACTOR
                row.append(score if c < b else jnp.where(causal, score, NEG))
            for c in range(ROWS // block):
                score = nt_dot(q, kp_ref[c * block : (c + 1) * block, lanes]) * FACTOR
                row.append(jnp.where(odd, score, NEG))
            scores.append(row)
        soft = [soften(row) for row in scores]
        stats = jnp.zeros((block, 128), jnp.float32)
        for head in heads:
            lanes = head_lanes(head)
            top, weights, total = soft[head]
            weights = [w.astype(jnp.bfloat16) for w in weights]
            out = jnp.dot(
                jnp.concatenate(weights[: b + 1], axis=1),
                v_ref[: (b + 1) * block, lanes],
                preferred_element_type=jnp.float32,
            ) + jnp.dot(
                jnp.concatenate(weights[b + 1 :], axis=1),
                vp_ref[:, lanes],
                preferred_element_type=jnp.float32,
            )
            out_ref[here, lanes] = out.astype(jnp.bfloat16)
            stats = stat_lanes(stats, head, top, total)
        packed_ref[here, :] = three_parts(stats)


def row_attend(parity, q, k, v, kp, vp):
    vmem = pl.BlockSpec(memory_space=pltpu.VMEM)
    return pl.pallas_call(
        row_kernel,
        out_shape=(
            jax.ShapeDtypeStruct((ROWS, WIDTH), jnp.bfloat16),
            jax.ShapeDtypeStruct((ROWS, 128), jnp.bfloat16),
        ),
        in_specs=[pl.BlockSpec(memory_space=pltpu.SMEM)] + [vmem] * 5,
        out_specs=(vmem, vmem),
        compiler_params=pltpu.CompilerParams(vmem_limit_bytes=VMEM),
        cost_estimate=LARGE,
        name="row_attend",
    )(parity, q, k, v, kp, vp)


def col_kernel(qkv_ref, out_ref):
    block = 128
    token = lax.broadcasted_iota(jnp.int32, (block, block), 0)
    other = lax.broadcasted_iota(jnp.int32, (block, block), 1)
    same = (token & (COLS - 1)) == (other & (COLS - 1))
    earlier = same & (other < token)
    heads = range(HEADS_HERE)

    def lanes(part, head):
        return slice(part * WIDTH + head * DH, part * WIDTH + (head + 1) * DH)

    for b in range(ROWS // block):
        here = slice(b * block, (b + 1) * block)
        scores = [
            [
                jnp.where(
                    same if c < b else earlier,
                    nt_dot(
                        qkv_ref[here, lanes(0, head)],
                        qkv_ref[c * block : (c + 1) * block, lanes(1, head)],
                    )
                    * FACTOR,
                    NEG,
                )
                for c in range(b + 1)
            ]
            for head in heads
        ]
        tops = [functools.reduce(jnp.maximum, scores[head]) for head in heads]
        tops = [jnp.maximum(jnp.max(top, axis=1, keepdims=True), NONE) for top in tops]
        weights = [[jnp.exp2(score - tops[head]) for score in scores[head]] for head in heads]
        totals = [
            jnp.sum(functools.reduce(jnp.add, weights[head]), axis=1, keepdims=True)
            for head in heads
        ]
        stats = jnp.zeros((block, 128), jnp.float32)
        for head in heads:
            out = jnp.dot(
                jnp.concatenate([w.astype(jnp.bfloat16) for w in weights[head]], axis=1),
                qkv_ref[: (b + 1) * block, lanes(2, head)],
                preferred_element_type=jnp.float32,
            )
            out_ref[here, head * DH : (head + 1) * DH] = out.astype(jnp.bfloat16)
            stats = stat_lanes(stats, head, tops[head], totals[head])
        out_ref[here, WIDTH:] = three_parts(stats)


def col_attend(qkv):
    return pl.pallas_call(
        col_kernel,
        out_shape=jax.ShapeDtypeStruct((ROWS, WIDTH + 128), jnp.bfloat16),
        in_specs=[pl.BlockSpec(memory_space=pltpu.VMEM)],
        out_specs=pl.BlockSpec(memory_space=pltpu.VMEM),
        compiler_params=pltpu.CompilerParams(vmem_limit_bytes=VMEM),
        cost_estimate=LARGE,
        name="col_attend",
    )(qkv)


def mix_kernel(row_ref, row_stat_ref, col_ref, out_ref):
    block = 128
    for b in range(ROWS // block):
        here = slice(b * block, (b + 1) * block)
        row_max, row_total = spread_stats(row_stat_ref[here, :])
        col_max, col_total = spread_stats(col_ref[here, WIDTH : WIDTH + 128])
        highest = jnp.maximum(row_max, col_max)
        row_factor = jnp.exp2(row_max - highest)
        col_factor = jnp.exp2(col_max - highest)
        row, col = (ref[here, :WIDTH].astype(jnp.float32) for ref in (row_ref, col_ref))
        mixed = row_factor * row + col_factor * col
        total = row_factor * row_total + col_factor * col_total
        out_ref[here, :] = (mixed / total).astype(jnp.bfloat16)


def mix(row_out, row_stat, col):
    vmem = pl.BlockSpec(memory_space=pltpu.VMEM)
    return pl.pallas_call(
        mix_kernel,
        out_shape=jax.ShapeDtypeStruct((ROWS, WIDTH), jnp.bfloat16),
        in_specs=[vmem] * 3,
        out_specs=vmem,
        compiler_params=pltpu.CompilerParams(vmem_limit_bytes=VMEM),
        cost_estimate=SMALL,
        name="mix",
    )(row_out, row_stat, col)


CHUNKS = 4
EARLY = ((0, 0), (0, 1), (1, 0), (1, 1), (3, 0), (3, 1))
LATE = ((2, 0), (2, 1))


def put_pieces(place_ref, pieces, origins, weight_ref, places):
    y, x, mp = place_ref[0], place_ref[1], place_ref[2]
    for (step, other), piece in zip(origins, pieces):
        there = (x + step) & 3
        lane = pl.multiple_of((2 * ((y + other) & 1) + there // 2) * DH, DH)
        for i in places:
            start = pl.multiple_of(i * 64 + (there & 1) * 32, 32)
            for group in range(N_MP):
                weight_ref[group ^ mp, pl.ds(start, 32), pl.ds(lane, DH)] = piece[group, i]


def arrange_kernel(place_ref, *refs):
    put_pieces(place_ref, refs[:-1], EARLY, refs[-1], range(16))


def arrange(place, pieces):
    vmem = pl.BlockSpec(memory_space=pltpu.VMEM)
    return pl.pallas_call(
        arrange_kernel,
        out_shape=jax.ShapeDtypeStruct((N_MP, PLANE * 32, WIDTH), jnp.bfloat16),
        in_specs=[pl.BlockSpec(memory_space=pltpu.SMEM)] + [vmem] * len(pieces),
        out_specs=vmem,
        compiler_params=pltpu.CompilerParams(vmem_limit_bytes=VMEM),
        cost_estimate=SMALL,
        name="arrange",
    )(place, *pieces)


def finish_kernel(place_ref, *refs):
    blocks, pieces = refs[:N_MP], refs[N_MP : N_MP + 2]
    out_ref, weight_ref, *results, done = refs[N_MP + 3 :]
    copies = []
    width = PLANE * 32 // CHUNKS
    for chunk in range(CHUNKS):
        here = slice(chunk * width, (chunk + 1) * width)
        part = 16 // CHUNKS
        put_pieces(place_ref, pieces, LATE, weight_ref, range(chunk * part, (chunk + 1) * part))
        total = None
        for j in range(N_MP):
            term = nt_dot(blocks[j][...], weight_ref[j, here, :])
            total = term if total is None else total + term
        results[chunk][...] = total.astype(jnp.bfloat16)
        copies.append(
            pltpu.make_async_copy(results[chunk], out_ref.at[:, here], done.at[chunk])
        )
        copies[-1].start()
    for copy in copies:
        copy.wait()


def finish(place, blocks, pieces, weight):
    vmem = pl.BlockSpec(memory_space=pltpu.VMEM)
    width = PLANE * 32 // CHUNKS
    inputs = (*blocks, *pieces, weight)
    return pl.pallas_call(
        finish_kernel,
        out_shape=(
            jax.ShapeDtypeStruct((ROWS, PLANE * 32), jnp.bfloat16),
            jax.ShapeDtypeStruct(weight.shape, weight.dtype),
        ),
        in_specs=[pl.BlockSpec(memory_space=pltpu.SMEM)] + [vmem] * len(inputs),
        out_specs=(pl.BlockSpec(memory_space=pl.ANY), vmem),
        input_output_aliases={len(inputs): 1},
        scratch_shapes=[pltpu.VMEM((ROWS, width), jnp.bfloat16)] * CHUNKS
        + [pltpu.SemaphoreType.DMA((CHUNKS,))],
        compiler_params=pltpu.CompilerParams(vmem_limit_bytes=VMEM),
        cost_estimate=SMALL,
        name="finish",
    )(place, *inputs)[0]


def same_parity():
    return [[i for i in range(N_SEQ) if i % 2 == p] for p in range(2)]


def swap_columns(value):
    return lax.all_to_all(
        value, "seq", split_axis=0, concat_axis=0, axis_index_groups=same_parity(), tiled=True
    )


def along(step, stride, size):
    pairs = []
    for i in range(N_SEQ):
        place = i // stride % size
        pairs.append((i, i + ((place + step) % size - place) * stride))
    return pairs


def turn(mine):
    pairs = []
    for seq in range(N_SEQ):
        z, place = divmod(seq, PLANE)
        for mp in range(N_MP):
            pairs.append((seq * N_MP + mp, (mp * PLANE + place) * N_MP + z))
    return lax.ppermute(mine, ("seq", "mp"), pairs)


def weight_messages(turned):
    heads = turned.reshape(4, 8, HEADS_HERE, DH).transpose(2, 1, 0, 3).reshape(1, 4 * 8, WIDTH)
    return jnp.broadcast_to(heads, (16, 4 * 8, WIDTH)).reshape(ROWS, WIDTH)


def weight_piece(received):
    tiles = received.reshape(64, 8, 4, DH).transpose(0, 2, 1, 3)
    return tiles.reshape(N_MP, 16, 32, DH)


def body(queries, keys, values, out_weight):
    seq, mp = lax.axis_index("seq"), lax.axis_index("mp")
    barrier = lax.optimization_barrier
    x_up, x_down = along(1, 1, 4), along(-1, 1, 4)
    y_pair = [(i, i ^ 4) for i in range(N_SEQ)]

    blank = jnp.zeros((ROWS, WIDTH), jnp.bfloat16)
    turned, together = barrier(
        (turn(out_weight.T), jnp.concatenate([queries, keys, values, blank], axis=1))
    )
    together = lax.dynamic_update_slice(together, weight_messages(turned), (0, 3 * WIDTH))
    arrived = swap_columns(together)

    to_odd = [(i, i + 1) for i in range(0, N_SEQ, 2)]
    keys_before = lax.ppermute(keys, "seq", to_odd)
    values_before = lax.ppermute(values, "seq", to_odd)

    own_0 = weight_piece(arrived[:, 3 * WIDTH :])
    own_1 = lax.ppermute(own_0, "seq", y_pair)

    col_own = col_attend(arrived)
    col_own, keys_before, values_before, own_0 = barrier(
        (col_own, keys_before, values_before, own_0)
    )
    less_0 = lax.ppermute(own_0, "seq", x_up)
    keys_before, values_before, own_0, own_1, less_0 = barrier(
        (keys_before, values_before, own_0, own_1, less_0)
    )
    more_0 = lax.ppermute(own_0, "seq", x_down)
    row_out, row_stat = row_attend(
        (seq % 2).astype(jnp.int32).reshape(1), queries, keys, values, keys_before, values_before
    )
    less_1 = lax.ppermute(own_1, "seq", x_up)
    more_1 = lax.ppermute(own_1, "seq", x_down)
    col = swap_columns(col_own)
    attended = mix(row_out, row_stat, col)

    near = [(i, i ^ 1) for i in range(N_MP)]
    far = [(i, i ^ 2) for i in range(N_MP)]
    across = lax.ppermute(attended, "mp", far)
    after, less_1, more_1 = barrier((attended, less_1, more_1))
    far_0 = lax.ppermute(less_0, "seq", x_up)
    far_1 = lax.ppermute(more_1, "seq", x_down)
    place = jnp.stack([seq // 4 % 8, seq % 4, mp]).astype(jnp.int32)
    weight = arrange(place, (own_0, own_1, more_0, more_1, less_0, less_1))
    after, weight = barrier((after, weight))
    beside = lax.ppermute(after, "mp", near)
    last = lax.ppermute(across, "mp", near)
    return finish(place, (after, beside, across, last), (far_0, far_1), weight)


def solution(mesh):
    placed = (P("seq", "mp"), P("seq", "mp"), P("seq", "mp"), P("mp", "seq"))
    return jax.shard_map(
        body, mesh=mesh, in_specs=placed, out_specs=P("seq", "mp"), check_vma=False
    )
```

```python
import functools

import jax
import jax.numpy as jnp
from jax import lax
from jax.experimental import pallas as pl
from jax.experimental.pallas import tpu as pltpu
from jax.sharding import PartitionSpec as P

DH = 128
HEADS_HERE = 4
ROWS = 512
WIDTH = HEADS_HERE * DH
N_MP = 4
N_SEQ = 128
PLANE = 32
COLS = 8
NEG = -1e30
NONE = -1e29
FACTOR = DH ** (-0.5) * 1.4426950408889634
VMEM = 40 * 1024 * 1024
SMALL = pl.CostEstimate(flops=1024, bytes_accessed=1024, transcendentals=0)
LARGE = pl.CostEstimate(flops=2 * 10**11, bytes_accessed=1024, transcendentals=0)

NT = (((1,), (1,)), ((), ()))


def nt_dot(a, b):
    return lax.dot_general(a, b, NT, preferred_element_type=jnp.float32)


def stat_lanes(old, head, largest, total):
    lane = lax.broadcasted_iota(jnp.int32, old.shape, 1)
    return jnp.where(lane == head, largest, jnp.where(lane == 4 + head, total, old))


def three_parts(stats):
    high = stats.astype(jnp.bfloat16).astype(jnp.float32)
    rest = stats - high
    middle = rest.astype(jnp.bfloat16).astype(jnp.float32)
    low = rest - middle
    parts = high + pltpu.roll(middle, 8, 1) + pltpu.roll(low, 16, 1)
    return parts.astype(jnp.bfloat16)


def spread_stats(stats):
    lane = lax.broadcasted_iota(jnp.int32, (128, WIDTH), 0)
    head = lax.broadcasted_iota(jnp.int32, (128, WIDTH), 1) // DH
    kept = lane < 24
    pick_max = jnp.where(kept & ((lane & 7) == head), 1.0, 0.0).astype(jnp.bfloat16)
    pick_total = jnp.where(kept & ((lane & 7) == head + 4), 1.0, 0.0).astype(jnp.bfloat16)
    largest = jnp.dot(stats, pick_max, preferred_element_type=jnp.float32)
    total = jnp.dot(stats, pick_total, preferred_element_type=jnp.float32)
    return largest, total


def head_lanes(head, part=0):
    return slice(part * WIDTH + head * DH, part * WIDTH + (head + 1) * DH)


def soften(scores):
    top = jnp.max(functools.reduce(jnp.maximum, scores), axis=1, keepdims=True)
    top = jnp.maximum(top, NONE)
    weights = [jnp.exp2(score - top) for score in scores]
    total = jnp.sum(functools.reduce(jnp.add, weights), axis=1, keepdims=True)
    return top, weights, total


def own_kernel(q_ref, k_ref, v_ref, out_ref, stat_ref):
    block = 128
    token = lax.broadcasted_iota(jnp.int32, (block, block), 0)
    other = lax.broadcasted_iota(jnp.int32, (block, block), 1)
    causal = other <= token
    heads = range(HEADS_HERE)
    for b in range(ROWS // block):
        here = slice(b * block, (b + 1) * block)
        scores = []
        for head in heads:
            lanes = head_lanes(head)
            row = []
            for c in range(b + 1):
                there = slice(c * block, (c + 1) * block)
                score = nt_dot(q_ref[here, lanes], k_ref[there, lanes]) * FACTOR
                row.append(score if c < b else jnp.where(causal, score, NEG))
            scores.append(row)
        soft = [soften(row) for row in scores]
        stats = jnp.zeros((block, 128), jnp.float32)
        for head in heads:
            lanes = head_lanes(head)
            top, weights, total = soft[head]
            out = jnp.dot(
                jnp.concatenate([w.astype(jnp.bfloat16) for w in weights], axis=1),
                v_ref[: (b + 1) * block, lanes],
                preferred_element_type=jnp.float32,
            )
            out_ref[here, lanes] = out.astype(jnp.bfloat16)
            stats = stat_lanes(stats, head, top, total)
        stat_ref[here, :] = stats


def before_kernel(parity_ref, q_ref, kp_ref, vp_ref, own_ref, stat_ref, out_ref, packed_ref):
    odd = parity_ref[0] == 1
    block = 128
    heads = range(HEADS_HERE)
    for b in range(ROWS // block):
        here = slice(b * block, (b + 1) * block)
        scores = []
        for head in heads:
            lanes = head_lanes(head)
            row = []
            for c in range(ROWS // block):
                there = slice(c * block, (c + 1) * block)
                score = nt_dot(q_ref[here, lanes], kp_ref[there, lanes]) * FACTOR
                row.append(jnp.where(odd, score, NEG))
            scores.append(row)
        soft = [soften(row) for row in scores]
        own_stats = stat_ref[here, :]
        stats = jnp.zeros((block, 128), jnp.float32)
        for head in heads:
            lanes = head_lanes(head)
            top, weights, total = soft[head]
            own_top = own_stats[:, head : head + 1]
            own_total = own_stats[:, 4 + head : 5 + head]
            highest = jnp.maximum(top, own_top)
            factor, own_factor = jnp.exp2(top - highest), jnp.exp2(own_top - highest)
            out = jnp.dot(
                jnp.concatenate([w.astype(jnp.bfloat16) for w in weights], axis=1),
                vp_ref[:, lanes],
                preferred_element_type=jnp.float32,
            )
            out = factor * out + own_factor * own_ref[here, lanes].astype(jnp.float32)
            out_ref[here, lanes] = out.astype(jnp.bfloat16)
            total = factor * total + own_factor * own_total
            stats = stat_lanes(stats, head, highest, total)
        packed_ref[here, :] = three_parts(stats)


def row_own(q, k, v):
    vmem = pl.BlockSpec(memory_space=pltpu.VMEM)
    return pl.pallas_call(
        own_kernel,
        out_shape=(
            jax.ShapeDtypeStruct((ROWS, WIDTH), jnp.bfloat16),
            jax.ShapeDtypeStruct((ROWS, 128), jnp.float32),
        ),
        in_specs=[vmem] * 3,
        out_specs=(vmem, vmem),
        compiler_params=pltpu.CompilerParams(vmem_limit_bytes=VMEM),
        cost_estimate=LARGE,
        name="row_own",
    )(q, k, v)


def row_before(parity, q, kp, vp, own, stats):
    vmem = pl.BlockSpec(memory_space=pltpu.VMEM)
    return pl.pallas_call(
        before_kernel,
        out_shape=(
            jax.ShapeDtypeStruct((ROWS, WIDTH), jnp.bfloat16),
            jax.ShapeDtypeStruct((ROWS, 128), jnp.bfloat16),
        ),
        in_specs=[pl.BlockSpec(memory_space=pltpu.SMEM)] + [vmem] * 5,
        out_specs=(vmem, vmem),
        compiler_params=pltpu.CompilerParams(vmem_limit_bytes=VMEM),
        cost_estimate=LARGE,
        name="row_before",
    )(parity, q, kp, vp, own, stats)


def col_kernel(qkv_ref, out_ref):
    block = 128
    token = lax.broadcasted_iota(jnp.int32, (block, block), 0)
    other = lax.broadcasted_iota(jnp.int32, (block, block), 1)
    same = (token & (COLS - 1)) == (other & (COLS - 1))
    earlier = same & (other < token)
    heads = range(HEADS_HERE)

    def lanes(part, head):
        return slice(part * WIDTH + head * DH, part * WIDTH + (head + 1) * DH)

    for b in range(ROWS // block):
        here = slice(b * block, (b + 1) * block)
        scores = [
            [
                jnp.where(
                    same if c < b else earlier,
                    nt_dot(
                        qkv_ref[here, lanes(0, head)],
                        qkv_ref[c * block : (c + 1) * block, lanes(1, head)],
                    )
                    * FACTOR,
                    NEG,
                )
                for c in range(b + 1)
            ]
            for head in heads
        ]
        tops = [functools.reduce(jnp.maximum, scores[head]) for head in heads]
        tops = [jnp.maximum(jnp.max(top, axis=1, keepdims=True), NONE) for top in tops]
        weights = [[jnp.exp2(score - tops[head]) for score in scores[head]] for head in heads]
        totals = [
            jnp.sum(functools.reduce(jnp.add, weights[head]), axis=1, keepdims=True)
            for head in heads
        ]
        stats = jnp.zeros((block, 128), jnp.float32)
        for head in heads:
            out = jnp.dot(
                jnp.concatenate([w.astype(jnp.bfloat16) for w in weights[head]], axis=1),
                qkv_ref[: (b + 1) * block, lanes(2, head)],
                preferred_element_type=jnp.float32,
            )
            out_ref[here, head * DH : (head + 1) * DH] = out.astype(jnp.bfloat16)
            stats = stat_lanes(stats, head, tops[head], totals[head])
        out_ref[here, WIDTH:] = three_parts(stats)


def col_attend(qkv):
    return pl.pallas_call(
        col_kernel,
        out_shape=jax.ShapeDtypeStruct((ROWS, WIDTH + 128), jnp.bfloat16),
        in_specs=[pl.BlockSpec(memory_space=pltpu.VMEM)],
        out_specs=pl.BlockSpec(memory_space=pltpu.VMEM),
        compiler_params=pltpu.CompilerParams(vmem_limit_bytes=VMEM),
        cost_estimate=LARGE,
        name="col_attend",
    )(qkv)


def mix_kernel(row_ref, row_stat_ref, col_ref, out_ref):
    block = 128
    for b in range(ROWS // block):
        here = slice(b * block, (b + 1) * block)
        row_max, row_total = spread_stats(row_stat_ref[here, :])
        col_max, col_total = spread_stats(col_ref[here, WIDTH : WIDTH + 128])
        highest = jnp.maximum(row_max, col_max)
        row_factor = jnp.exp2(row_max - highest)
        col_factor = jnp.exp2(col_max - highest)
        row, col = (ref[here, :WIDTH].astype(jnp.float32) for ref in (row_ref, col_ref))
        mixed = row_factor * row + col_factor * col
        total = row_factor * row_total + col_factor * col_total
        out_ref[here, :] = (mixed / total).astype(jnp.bfloat16)


def mix(row_out, row_stat, col):
    vmem = pl.BlockSpec(memory_space=pltpu.VMEM)
    return pl.pallas_call(
        mix_kernel,
        out_shape=jax.ShapeDtypeStruct((ROWS, WIDTH), jnp.bfloat16),
        in_specs=[vmem] * 3,
        out_specs=vmem,
        compiler_params=pltpu.CompilerParams(vmem_limit_bytes=VMEM),
        cost_estimate=SMALL,
        name="mix",
    )(row_out, row_stat, col)


CHUNKS = 4
EARLY = ((0, 0), (0, 1), (1, 0), (1, 1), (3, 0), (3, 1))
LATE = ((2, 0), (2, 1))


def put_pieces(place_ref, pieces, origins, weight_ref, places):
    y, x, mp = place_ref[0], place_ref[1], place_ref[2]
    for (step, other), piece in zip(origins, pieces):
        there = (x + step) & 3
        lane = pl.multiple_of((2 * ((y + other) & 1) + there // 2) * DH, DH)
        for i in places:
            start = pl.multiple_of(i * 64 + (there & 1) * 32, 32)
            for group in range(N_MP):
                weight_ref[group ^ mp, pl.ds(start, 32), pl.ds(lane, DH)] = piece[group, i]


def arrange_kernel(place_ref, *refs):
    put_pieces(place_ref, refs[:-1], EARLY, refs[-1], range(16))


def arrange(place, pieces):
    vmem = pl.BlockSpec(memory_space=pltpu.VMEM)
    return pl.pallas_call(
        arrange_kernel,
        out_shape=jax.ShapeDtypeStruct((N_MP, PLANE * 32, WIDTH), jnp.bfloat16),
        in_specs=[pl.BlockSpec(memory_space=pltpu.SMEM)] + [vmem] * len(pieces),
        out_specs=vmem,
        compiler_params=pltpu.CompilerParams(vmem_limit_bytes=VMEM),
        cost_estimate=SMALL,
        name="arrange",
    )(place, *pieces)


def finish_kernel(place_ref, *refs):
    blocks, pieces = refs[:N_MP], refs[N_MP : N_MP + 2]
    out_ref, weight_ref, *results, done = refs[N_MP + 3 :]
    copies = []
    width = PLANE * 32 // CHUNKS
    for chunk in range(CHUNKS):
        here = slice(chunk * width, (chunk + 1) * width)
        part = 16 // CHUNKS
        put_pieces(place_ref, pieces, LATE, weight_ref, range(chunk * part, (chunk + 1) * part))
        total = None
        for j in range(N_MP):
            term = nt_dot(blocks[j][...], weight_ref[j, here, :])
            total = term if total is None else total + term
        results[chunk][...] = total.astype(jnp.bfloat16)
        copies.append(
            pltpu.make_async_copy(results[chunk], out_ref.at[:, here], done.at[chunk])
        )
        copies[-1].start()
    for copy in copies:
        copy.wait()


def finish(place, blocks, pieces, weight):
    vmem = pl.BlockSpec(memory_space=pltpu.VMEM)
    width = PLANE * 32 // CHUNKS
    inputs = (*blocks, *pieces, weight)
    return pl.pallas_call(
        finish_kernel,
        out_shape=(
            jax.ShapeDtypeStruct((ROWS, PLANE * 32), jnp.bfloat16),
            jax.ShapeDtypeStruct(weight.shape, weight.dtype),
        ),
        in_specs=[pl.BlockSpec(memory_space=pltpu.SMEM)] + [vmem] * len(inputs),
        out_specs=(pl.BlockSpec(memory_space=pl.ANY), vmem),
        input_output_aliases={len(inputs): 1},
        scratch_shapes=[pltpu.VMEM((ROWS, width), jnp.bfloat16)] * CHUNKS
        + [pltpu.SemaphoreType.DMA((CHUNKS,))],
        compiler_params=pltpu.CompilerParams(vmem_limit_bytes=VMEM),
        cost_estimate=SMALL,
        name="finish",
    )(place, *inputs)[0]


def same_parity():
    return [[i for i in range(N_SEQ) if i % 2 == p] for p in range(2)]


def swap_columns(value):
    return lax.all_to_all(
        value, "seq", split_axis=0, concat_axis=0, axis_index_groups=same_parity(), tiled=True
    )


def along(step, stride, size):
    pairs = []
    for i in range(N_SEQ):
        place = i // stride % size
        pairs.append((i, i + ((place + step) % size - place) * stride))
    return pairs


def turn(mine):
    pairs = []
    for seq in range(N_SEQ):
        z, place = divmod(seq, PLANE)
        for mp in range(N_MP):
            pairs.append((seq * N_MP + mp, (mp * PLANE + place) * N_MP + z))
    return lax.ppermute(mine, ("seq", "mp"), pairs)


def weight_messages(turned):
    heads = turned.reshape(4, 8, HEADS_HERE, DH).transpose(2, 1, 0, 3).reshape(1, 4 * 8, WIDTH)
    return jnp.broadcast_to(heads, (16, 4 * 8, WIDTH)).reshape(ROWS, WIDTH)


def weight_piece(received):
    tiles = received.reshape(64, 8, 4, DH).transpose(0, 2, 1, 3)
    return tiles.reshape(N_MP, 16, 32, DH)


def body(queries, keys, values, out_weight):
    seq, mp = lax.axis_index("seq"), lax.axis_index("mp")
    barrier = lax.optimization_barrier
    x_up, x_down = along(1, 1, 4), along(-1, 1, 4)
    y_pair = [(i, i ^ 4) for i in range(N_SEQ)]

    blank = jnp.zeros((ROWS, WIDTH), jnp.bfloat16)
    turned, together = barrier(
        (turn(out_weight.T), jnp.concatenate([queries, keys, values, blank], axis=1))
    )
    together = lax.dynamic_update_slice(together, weight_messages(turned), (0, 3 * WIDTH))
    arrived = swap_columns(together)

    to_odd = [(i, i + 1) for i in range(0, N_SEQ, 2)]
    keys_before = lax.ppermute(keys, "seq", to_odd)
    values_before = lax.ppermute(values, "seq", to_odd)

    half_out, half_stat = row_own(queries, keys, values)
    arrived, half_out, half_stat = barrier((arrived, half_out, half_stat))
    own_0 = weight_piece(arrived[:, 3 * WIDTH :])
    own_1 = lax.ppermute(own_0, "seq", y_pair)

    col_own = col_attend(arrived)
    col_own, keys_before, values_before, own_0 = barrier(
        (col_own, keys_before, values_before, own_0)
    )
    less_0 = lax.ppermute(own_0, "seq", x_up)
    keys_before, values_before, own_0, own_1, less_0 = barrier(
        (keys_before, values_before, own_0, own_1, less_0)
    )
    more_0 = lax.ppermute(own_0, "seq", x_down)
    parity = (seq % 2).astype(jnp.int32).reshape(1)
    row_out, row_stat = row_before(
        parity, queries, keys_before, values_before, half_out, half_stat
    )
    less_1 = lax.ppermute(own_1, "seq", x_up)
    more_1 = lax.ppermute(own_1, "seq", x_down)
    col = swap_columns(col_own)
    attended = mix(row_out, row_stat, col)

    near = [(i, i ^ 1) for i in range(N_MP)]
    far = [(i, i ^ 2) for i in range(N_MP)]
    across = lax.ppermute(attended, "mp", far)
    after, less_1, more_1 = barrier((attended, less_1, more_1))
    far_0 = lax.ppermute(less_0, "seq", x_up)
    far_1 = lax.ppermute(more_1, "seq", x_down)
    place = jnp.stack([seq // 4 % 8, seq % 4, mp]).astype(jnp.int32)
    weight = arrange(place, (own_0, own_1, more_0, more_1, less_0, less_1))
    after, weight = barrier((after, weight))
    beside = lax.ppermute(after, "mp", near)
    last = lax.ppermute(across, "mp", near)
    return finish(place, (after, beside, across, last), (far_0, far_1), weight)


def solution(mesh):
    placed = (P("seq", "mp"), P("seq", "mp"), P("seq", "mp"), P("mp", "seq"))
    return jax.shard_map(
        body, mesh=mesh, in_specs=placed, out_specs=P("seq", "mp"), check_vma=False
    )
```
